256 devices in a mesh: fsdp: 32 (over z, y_hi, core), sp: 8 (over x, y_lo).
Axes of the slice: x: 4, y: 4 (y_hi: 2, y_lo: 2; y = y_hi * 2 + y_lo), z: 8, core: 2. Of those that a mesh axis runs over, the one named last changes fastest.
Arguments:
- tokens_in: bfloat16 [32768, 4096], P(('fsdp', 'sp')), may hold values from -8 to 8
- queries: bfloat16 [32768, 5120], P(('fsdp', 'sp')), may hold values from -4000 to 4000
- kv_weight: bfloat16 [4096, 1024], P(('fsdp', 'sp')), may hold values from -0.4 to 0.4
- value_head_matrix: float32 [5120], P('sp'), may hold values from -5 to 5
- packed_episode_lengths: int32 [32, 4], P('fsdp'), may hold values from 1 to 512, 1024 in all within a row
- value_target_positions: int32 [32, 256], P('fsdp'), may hold values from 0 to 1023
- returns: float32 [32, 256], P('fsdp'), may hold values from -8 to 8
Outputs:
- query_grad: bfloat16 [32768, 5120], P(('fsdp', 'sp'))
- input_grad: bfloat16 [32768, 4096], P(('fsdp', 'sp'))
- kv_weight_grad: float32 [4096, 1024], P(('fsdp', 'sp'))
The draws below stay inside these ranges and needn't reach their ends.
Inputs may be any that keep to these rules, and one draw needn't show every extreme that they name: `packed_episode_lengths`: each slab's lengths add up to 1024.
All inputs are finite; a program needn't handle non-finite values.
Results may differ from the reference program's by a relative error of at most 0.014.
Values may be sent and summed in bfloat16 or wider, within the bound.
A program may use at most 128 MiB of HBM per device.

```python
import math
from functools import partial
import jax
import jax.numpy as jnp
import numpy as np
from jax import lax

FEATURE_PART = 4096
QUERY_HEAD_PART = 40
KEY_VALUE_HEADS = 4
HEAD_SIZE = 128
EPIS = 4
SLAB_TOKENS = 1024
SLAB_COUNT = 32
TOKEN_COUNT = 32768
TARGETS = 256


def outlier_rows(key):
    slab_keys = jax.random.split(jax.random.fold_in(key, 301), SLAB_COUNT)
    return jax.vmap(lambda sub_key: jax.random.permutation(sub_key, SLAB_TOKENS - 2)[:3] + 1)(slab_keys)


def token_field(key):
    return jnp.clip(jax.random.normal(jax.random.fold_in(key, 101), (TOKEN_COUNT, FEATURE_PART), jnp.float32), -6.0, 6.0)


def weight_field(key):
    base_offset = jnp.clip(jax.random.normal(jax.random.fold_in(key, 201), (FEATURE_PART, 2 * KEY_VALUE_HEADS * HEAD_SIZE), jnp.float32), -6.0, 6.0)
    return base_offset / jnp.sqrt(jnp.float32(FEATURE_PART))


def draw_tokens_in(key, part):
    return token_field(key).astype(jnp.bfloat16)


def draw_kv_weight(key, part):
    return weight_field(key).astype(jnp.bfloat16)


def draw_queries(key, part):
    base_offset = jnp.clip(jax.random.normal(jax.random.fold_in(key, 401), (TOKEN_COUNT, QUERY_HEAD_PART * HEAD_SIZE), jnp.float32), -6.0, 6.0)
    return base_offset.astype(jnp.bfloat16)


def draw_value_target_positions(key, part):
    excluded = jnp.sort(outlier_rows(key), axis=1)
    drawn = jax.random.randint(jax.random.fold_in(key, 601), (SLAB_COUNT, TARGETS), 0, SLAB_TOKENS - 3)
    for column in range(3):
        drawn = drawn + (drawn >= excluded[:, column:column + 1]).astype(jnp.int32)
    drawn = drawn.at[:, 0].set(0)
    drawn = drawn.at[:, 1].set(SLAB_TOKENS - 1)
    return drawn.astype(jnp.int32)


def draw_value_head_matrix(key, part):
    heads = (jnp.arange(QUERY_HEAD_PART * HEAD_SIZE, dtype=jnp.int32) // HEAD_SIZE).astype(jnp.float32)
    rising = 1.0 + 2.0 * heads / max(QUERY_HEAD_PART - 1, 1)
    noise = jnp.clip(jax.random.normal(jax.random.fold_in(key, 501), (QUERY_HEAD_PART * HEAD_SIZE,), jnp.float32), -4.0, 4.0)
    return (0.25 * noise * rising).astype(jnp.float32)


def steps_of(rng, shape, cuts, least, high):
    level = 1.0
    for axis_at, blocks in cuts:
        heights = jax.random.uniform(jax.random.fold_in(jax.random.fold_in(rng, 6), axis_at), (blocks,), jnp.float32, least / len(cuts), high / len(cuts))
        level = level * jnp.repeat(jnp.exp(heights), shape[axis_at] // blocks).reshape((-1,) + (1,) * (len(shape) - 1 - axis_at))
    return level


def length_profile(count, total, most, slope):
    portions = [(1 << 20) // math.isqrt(grade ** slope) + 1 for grade in range(2, count + 1)]
    surplus, given = total - most - (count - 1), [1] * (count - 1)
    while surplus > 0:
        free = [i for i in range(count - 1) if given[i] < most]
        mass, budget = sum([portions[i] for i in free]), surplus
        for i in free:
            more = min(most - given[i], max(1, budget * portions[i] // mass), surplus)
            given[i] = given[i] + more
            surplus = surplus - more
    return np.array([most] + given)


def ragged(rng, number_of, total, reach, slope):
    if number_of == 2:
        one = jax.random.randint(rng, (), max(1, total - reach), min(reach, total - 1) + 1)
        return jnp.stack([one, total - one])
    sizes = jnp.asarray(length_profile(number_of, total, reach, slope), jnp.int32)
    pairs = (number_of - 1) // 2
    donor, sink = sizes[1:1 + 2 * pairs:2], sizes[2:2 + 2 * pairs:2]
    margin = jnp.minimum(donor - 1, reach - sink)
    shifted = jax.random.randint(jax.random.fold_in(rng, 1), (pairs,), 0, 1 << 20) % (margin + 1)
    sizes = sizes.at[1:1 + 2 * pairs:2].set(donor - shifted).at[2:2 + 2 * pairs:2].set(sink + shifted)
    return sizes[jax.random.permutation(jax.random.fold_in(rng, 2), number_of)]


def normal_values(own_key, extent, width, limit, shards=(), kind=jnp.bfloat16):
    values = jax.random.normal(own_key, extent, jnp.float32) * width
    if len(shards) > 0:
        values = steps_of(own_key, extent, shards, -0.22, 0.18) * values
    return jnp.clip(values, min=-limit, max=limit).astype(kind)


def setup_inputs(seed: int = 0) -> dict:
    seeds = jax.random.split(jax.random.key(seed), 8)
    return {
        "tokens_in": draw_tokens_in(jax.random.fold_in(seeds[7], 71), 0),
        "queries": draw_queries(jax.random.fold_in(seeds[7], 71), 0),
        "kv_weight": draw_kv_weight(jax.random.fold_in(seeds[7], 71), 0),
        "value_head_matrix": draw_value_head_matrix(jax.random.fold_in(seeds[7], 71), 0),
        "packed_episode_lengths": jax.vmap(lambda own: ragged(own, EPIS, SLAB_TOKENS, SLAB_TOKENS // 2, 2))(jax.random.split(seeds[4], SLAB_COUNT)).reshape((SLAB_COUNT, EPIS)).astype(jnp.int32),
        "value_target_positions": draw_value_target_positions(jax.random.fold_in(seeds[7], 71), 0),
        "returns": normal_values(seeds[6], (SLAB_COUNT, TARGETS), 2.0, 8.0, ((0, 32),), jnp.float32),
    }


neg_fill = -1e+30

def episode_index(lengths):
    bounds = jnp.cumsum(lengths)
    places = lax.broadcasted_iota(jnp.int32, (SLAB_TOKENS, bounds.shape[0]), 0)
    return lax.optimization_barrier(jnp.sum((places >= bounds[None, :]).astype(jnp.int32), axis=1))

def slab_pass(value_head_matrix, inputs_of_slab):
    rows_of_query, key_value_rows, lengths, positions, targets = inputs_of_slab
    query_group_size = QUERY_HEAD_PART // KEY_VALUE_HEADS
    score_scale = 1.0 / math.sqrt(HEAD_SIZE)
    queries_wide_float = rows_of_query.astype(jnp.float32).reshape(SLAB_TOKENS, KEY_VALUE_HEADS, query_group_size, HEAD_SIZE)
    keys_wide_float = key_value_rows[:, :KEY_VALUE_HEADS * HEAD_SIZE].astype(jnp.float32).reshape(SLAB_TOKENS, KEY_VALUE_HEADS, HEAD_SIZE)
    values_wide_float = key_value_rows[:, KEY_VALUE_HEADS * HEAD_SIZE:].astype(jnp.float32).reshape(SLAB_TOKENS, KEY_VALUE_HEADS, HEAD_SIZE)
    value_readout = value_head_matrix.reshape(KEY_VALUE_HEADS, query_group_size, HEAD_SIZE)
    episode = episode_index(lengths)
    places = lax.broadcasted_iota(jnp.int32, (SLAB_TOKENS,), 0)
    allowed = (episode[:, None] == episode[None, :]) & (places[None, :] <= places[:, None])
    raw_scores = jnp.einsum('qcgd,kcd->cgqk', queries_wide_float, keys_wide_float) * score_scale
    masked = jnp.where(allowed[None, None], raw_scores, neg_fill)
    row_max = lax.optimization_barrier(jnp.max(masked, axis=-1))
    weights = jnp.exp(masked - row_max[..., None])
    prob_rows = weights / lax.optimization_barrier(jnp.sum(weights, axis=-1))[..., None]
    probs_low = lax.optimization_barrier(prob_rows.astype(jnp.bfloat16)).astype(jnp.float32)
    attended = jnp.einsum('cgqk,kcd->qcgd', probs_low, values_wide_float)
    head_value = lax.optimization_barrier(jnp.sum(attended * value_readout[None], axis=-1))
    estimate = lax.optimization_barrier(jnp.sum(head_value, axis=(1, 2)))[positions]
    row_coef = jnp.zeros((SLAB_TOKENS,), jnp.float32).at[positions].add(estimate - targets)
    grad_out = lax.optimization_barrier((row_coef[:, None, None, None] * value_readout[None]).astype(jnp.bfloat16)).astype(jnp.float32)
    delta_all = jnp.transpose(row_coef[:, None, None] * head_value, (1, 2, 0))
    grad_probs = jnp.einsum('qcgd,kcd->cgqk', grad_out, values_wide_float)
    grad_scores = lax.optimization_barrier((prob_rows * (grad_probs - delta_all[..., None])).astype(jnp.bfloat16)).astype(jnp.float32)
    query_grad = (jnp.einsum('cgqk,kcd->qcgd', grad_scores, keys_wide_float) * score_scale).astype(jnp.bfloat16)
    key_gradient = jnp.einsum('cgqk,qcgd->kcd', grad_scores, queries_wide_float) * score_scale
    value_gradient = jnp.einsum('cgqk,qcgd->kcd', probs_low, grad_out)
    key_value_gradient_rows = jnp.concatenate([key_gradient.reshape(SLAB_TOKENS, KEY_VALUE_HEADS * HEAD_SIZE), value_gradient.reshape(SLAB_TOKENS, KEY_VALUE_HEADS * HEAD_SIZE)], axis=1).astype(jnp.bfloat16)
    return (query_grad.reshape(SLAB_TOKENS, QUERY_HEAD_PART * HEAD_SIZE), key_value_gradient_rows)

def reference(tokens_in, queries, kv_weight, value_head_matrix, packed_episode_lengths, value_target_positions, returns):
    key_value_rows = jnp.dot(tokens_in, kv_weight, preferred_element_type=jnp.float32).astype(jnp.bfloat16)
    inputs_of_slab = (queries.reshape(SLAB_COUNT, SLAB_TOKENS, QUERY_HEAD_PART * HEAD_SIZE), key_value_rows.reshape(SLAB_COUNT, SLAB_TOKENS, 2 * KEY_VALUE_HEADS * HEAD_SIZE), packed_episode_lengths, value_target_positions, returns)
    query_grad, key_value_gradient_rows = lax.map(partial(slab_pass, value_head_matrix), inputs_of_slab)
    key_value_gradient_rows = key_value_gradient_rows.reshape(TOKEN_COUNT, 2 * KEY_VALUE_HEADS * HEAD_SIZE)
    input_grad = jnp.dot(key_value_gradient_rows, kv_weight.T, preferred_element_type=jnp.float32).astype(jnp.bfloat16)
    weight_grad = jnp.dot(tokens_in.T, key_value_gradient_rows, preferred_element_type=jnp.float32)
    return (query_grad.reshape(TOKEN_COUNT, QUERY_HEAD_PART * HEAD_SIZE), input_grad, weight_grad)
```

```python
import math

import jax
import jax.numpy as jnp
from jax import lax
from jax.experimental import pallas as pl
from jax.experimental.pallas import tpu as pltpu
from jax.sharding import PartitionSpec as P

HEADS = 40
KV = 4
GROUP = 10
D = 128
SCALE = 1.0 / math.sqrt(D)
ROWS = 128
WIN = 640
TILE = 32
NEG = -1e30
HIGH = lax.Precision.HIGHEST


def tdot(a, b, precision=None):
    return lax.dot_general(
        a, b, (((0,), (0,)), ((), ())), precision=precision, preferred_element_type=jnp.float32
    )


def ndot(a, b):
    return lax.dot_general(a, b, (((1,), (1,)), ((), ())), preferred_element_type=jnp.float32)


def attention_kernel(
    base_ref, len_ref, pos_ref, ret_ref, q_ref, k_ref, u_ref, dq_ref, dk_ref, w_ref,
    qc, dqc, props, probs, heads,
):
    base = base_ref[0]
    rows = base + lax.broadcasted_iota(jnp.int32, (ROWS, 1), 0)
    hits = (rows == pos_ref[...]).astype(jnp.float32)
    count = jnp.sum(hits, axis=1, keepdims=True)
    total_ret = jnp.sum(hits * ret_ref[...], axis=1, keepdims=True)
    marked = (count > 0).astype(jnp.float32)
    tri = (
        lax.broadcasted_iota(jnp.int32, (ROWS, ROWS), 1)
        <= lax.broadcasted_iota(jnp.int32, (ROWS, ROWS), 0)
    ).astype(jnp.bfloat16)
    rank = jnp.dot(
        tri, jnp.broadcast_to(marked, (ROWS, D)).astype(jnp.bfloat16),
        preferred_element_type=jnp.float32,
    )
    n = jnp.sum(marked).astype(jnp.int32)
    slots = lax.broadcasted_iota(jnp.int32, (ROWS, ROWS), 1)
    pick = ((rank.astype(jnp.int32) - 1 == slots) & (marked > 0)).astype(jnp.float32)
    lane = lax.broadcasted_iota(jnp.int32, (ROWS, D), 1)
    b1 = len_ref[0, 0]
    b2 = b1 + len_ref[0, 1]
    b3 = b2 + len_ref[0, 2]
    start = jnp.where(rows >= b3, b3, jnp.where(rows >= b2, b2, jnp.where(rows >= b1, b1, 0)))
    fields = jnp.where(lane == 0, count, 0.0)
    fields = jnp.where(lane == 1, total_ret, fields)
    fields = jnp.where(lane == 2, rows.astype(jnp.float32), fields)
    fields = jnp.where(lane == 3, start.astype(jnp.float32), fields)
    props[...] = tdot(pick, fields, HIGH)
    pick_low = pick.astype(jnp.bfloat16)
    qc[...] = tdot(pick_low, q_ref[...]).astype(jnp.bfloat16)
    dqc[...] = jnp.zeros_like(dqc)
    dk_ref[...] = jnp.zeros_like(dk_ref)
    w_ref[...] = jnp.zeros_like(w_ref)
    places = (base - 512) + lax.broadcasted_iota(jnp.int32, (1, WIN), 1)

    @pl.loop(0, (n + TILE - 1) // TILE)
    def _(t):
        at = pl.ds(pl.multiple_of(t * TILE, TILE), TILE)
        prop = props[at, :]
        cnt, ret = prop[:, 0:1], prop[:, 1:2]
        row, low = prop[:, 2:3].astype(jnp.int32), prop[:, 3:4].astype(jnp.int32)
        allowed = (places >= low) & (places <= row)
        estimate = jnp.zeros((TILE, 1), jnp.float32)
        for c in range(KV):
            keys = k_ref[:, c * D : (c + 1) * D]
            q = jnp.concatenate(
                [qc[at, (c * GROUP + g) * D : (c * GROUP + g + 1) * D] for g in range(GROUP)], axis=0
            )
            scores = ndot(q, keys) * SCALE
            for g in range(GROUP):
                h = c * GROUP + g
                s = jnp.where(allowed, scores[g * TILE : (g + 1) * TILE, :], NEG)
                e = jnp.exp(s - jnp.max(s, axis=1, keepdims=True))
                p = e / jnp.sum(e, axis=1, keepdims=True)
                probs[h] = p
                low_p = p.astype(jnp.bfloat16).astype(jnp.float32)
                hv = jnp.sum(low_p * u_ref[h : h + 1, :], axis=1, keepdims=True)
                heads[h] = hv
                estimate = estimate + hv
        coef = cnt * estimate - ret
        for c in range(KV):
            keys = k_ref[:, c * D : (c + 1) * D]
            q = jnp.concatenate(
                [qc[at, (c * GROUP + g) * D : (c * GROUP + g + 1) * D] for g in range(GROUP)], axis=0
            )
            parts = []
            for g in range(GROUP):
                h = c * GROUP + g
                p = probs[h]
                low_p = p.astype(jnp.bfloat16).astype(jnp.float32)
                w_ref[h : h + 1, :] += jnp.sum(low_p * coef, axis=0, keepdims=True)
                parts.append(
                    (p * (coef * u_ref[h : h + 1, :] - coef * heads[h])).astype(jnp.bfloat16)
                )
            gs = jnp.concatenate(parts, axis=0)
            dq = (jnp.dot(gs, keys, preferred_element_type=jnp.float32) * SCALE).astype(jnp.bfloat16)
            for g in range(GROUP):
                h = c * GROUP + g
                dqc[at, h * D : (h + 1) * D] = dq[g * TILE : (g + 1) * TILE, :]
            dk_ref[:, c * D : (c + 1) * D] += tdot(gs, q) * SCALE

    dq_ref[...] = jnp.dot(
        pick_low, dqc[...], preferred_element_type=jnp.float32
    ).astype(jnp.bfloat16)


def attention(base, lengths, positions, returns, queries, keys, u):
    vmem = pl.BlockSpec(memory_space=pltpu.VMEM)
    smem = pl.BlockSpec(memory_space=pltpu.SMEM)
    return pl.pallas_call(
        attention_kernel,
        out_shape=(
            jax.ShapeDtypeStruct((ROWS, HEADS * D), jnp.bfloat16),
            jax.ShapeDtypeStruct((WIN, KV * D), jnp.float32),
            jax.ShapeDtypeStruct((HEADS, WIN), jnp.float32),
        ),
        in_specs=[smem, smem, vmem, vmem, vmem, vmem, vmem],
        out_specs=(vmem, vmem, vmem),
        scratch_shapes=[
            pltpu.VMEM((ROWS, HEADS * D), jnp.bfloat16),
            pltpu.VMEM((ROWS, HEADS * D), jnp.bfloat16),
            pltpu.VMEM((ROWS, D), jnp.float32),
            pltpu.VMEM((HEADS, TILE, WIN), jnp.float32),
            pltpu.VMEM((HEADS, TILE, 1), jnp.float32),
        ],
        compiler_params=pltpu.CompilerParams(vmem_limit_bytes=48 * 2**20),
    )(base, lengths, positions, returns, queries, keys, u)


def block_diagonal(vhm):
    head_kv = lax.broadcasted_iota(jnp.int32, (HEADS, KV, 1), 0) // GROUP
    kv = lax.broadcasted_iota(jnp.int32, (HEADS, KV, 1), 1)
    return jnp.where(head_kv == kv, vhm.reshape(HEADS, 1, D), 0.0).reshape(HEADS, KV * D)


def split(x):
    hi = x.astype(jnp.bfloat16)
    return hi, (x - hi.astype(jnp.float32)).astype(jnp.bfloat16)


def on_device(tokens, queries, kv_weight, vhm, lengths, positions, returns):
    sp = lax.axis_index("sp")
    base = sp * ROWS
    readout = block_diagonal(lax.all_gather(vhm, "sp", axis=0, tiled=True))
    wv = kv_weight[:, KV * D :].astype(jnp.float32)
    folded = lax.dot_general(
        wv, readout, (((1,), (1,)), ((), ())), precision=HIGH, preferred_element_type=jnp.float32
    )
    hi, lo = split(folded)
    mine = jnp.concatenate(
        [kv_weight[:, : KV * D], hi, lo, jnp.zeros((hi.shape[0], D - 2 * HEADS), jnp.bfloat16)], axis=1
    )
    weight = lax.all_gather(mine, ("fsdp", "sp"), axis=0, tiled=True)
    rows = jnp.dot(tokens, weight, preferred_element_type=jnp.float32)
    k_mine = rows[:, : KV * D].astype(jnp.bfloat16)
    u_mine = (rows[:, 512:552] + rows[:, 552:592]).T
    k_all = jnp.pad(lax.all_gather(k_mine, "sp", axis=0, tiled=True), ((512, 0), (0, 0)))
    u_all = jnp.pad(lax.all_gather(u_mine, "sp", axis=1, tiled=True), ((0, 0), (512, 0)))
    k_win = lax.dynamic_slice_in_dim(k_all, base, WIN, 0)
    u_win = lax.dynamic_slice_in_dim(u_all, base, WIN, 1)
    dq, dk, w = attention(base.reshape(1), lengths, positions, returns, queries, k_win, u_win)
    part = jnp.concatenate([dk, w.T], axis=1)
    whole = lax.dynamic_update_slice_in_dim(
        jnp.zeros((1536, 552), jnp.float32), part, base, 0
    )[512:]
    grad = lax.psum_scatter(whole, "sp", scatter_dimension=0, tiled=True)
    k_grad = grad[:, :512].astype(jnp.bfloat16)
    w_hi, w_lo = split(grad[:, 512:])
    pad = jnp.zeros((ROWS, D - 3 * HEADS), jnp.bfloat16)
    left = jnp.concatenate([k_grad, w_hi, w_lo, w_hi, pad], axis=1)
    right = jnp.concatenate([weight[:, :552], weight[:, 512:592], weight[:, 592:600]], axis=1)
    input_grad = lax.dot_general(
        left, right, (((1,), (1,)), ((), ())), preferred_element_type=jnp.float32
    ).astype(jnp.bfloat16)
    outer = tdot(tokens, left[:, :592])
    outer = jnp.concatenate([outer[:, :512], outer[:, 512:552] + outer[:, 552:592]], axis=1)
    mine_grad = lax.psum_scatter(outer, ("fsdp", "sp"), scatter_dimension=0, tiled=True)
    v_grad = jnp.dot(
        mine_grad[:, 512:], readout, precision=HIGH, preferred_element_type=jnp.float32
    )
    return dq, input_grad, jnp.concatenate([mine_grad[:, :512], v_grad], axis=1)


def solution(mesh):
    rows = P(("fsdp", "sp"), None)
    slab = P("fsdp", None)
    return jax.shard_map(
        on_device,
        mesh=mesh,
        in_specs=(rows, rows, rows, P("sp"), slab, slab, slab),
        out_specs=(rows, rows, rows),
        check_vma=False,
    )
```

```python
import math

import jax
import jax.numpy as jnp
from jax import lax
from jax.experimental import pallas as pl
from jax.experimental.pallas import tpu as pltpu
from jax.sharding import PartitionSpec as P

HEADS = 40
KV = 4
GROUP = 10
D = 128
SCALE = 1.0 / math.sqrt(D)
ROWS = 128
WIN = 640
TILE = 32
NEG = -1e30
HIGH = lax.Precision.HIGHEST


def tdot(a, b, precision=None):
    return lax.dot_general(
        a, b, (((0,), (0,)), ((), ())), precision=precision, preferred_element_type=jnp.float32
    )


def ndot(a, b):
    return lax.dot_general(a, b, (((1,), (1,)), ((), ())), preferred_element_type=jnp.float32)


def attention_kernel(
    len_ref, pos_ref, ret_ref, q_ref, k_ref, vhm_ref, dq_ref, far_ref, near_ref, w_ref,
    qc, dqc, props, probs, heads, dk_ref, u_ref,
):
    base = lax.axis_index("sp") * ROWS
    rows = base + lax.broadcasted_iota(jnp.int32, (ROWS, 1), 0)
    hits = (rows == pos_ref[...]).astype(jnp.float32)
    count = jnp.sum(hits, axis=1, keepdims=True)
    total_ret = jnp.sum(hits * ret_ref[...], axis=1, keepdims=True)
    marked = (count > 0).astype(jnp.float32)
    tri = (
        lax.broadcasted_iota(jnp.int32, (ROWS, ROWS), 1)
        <= lax.broadcasted_iota(jnp.int32, (ROWS, ROWS), 0)
    ).astype(jnp.bfloat16)
    rank = jnp.dot(
        tri, jnp.broadcast_to(marked, (ROWS, D)).astype(jnp.bfloat16),
        preferred_element_type=jnp.float32,
    )
    n = jnp.sum(marked).astype(jnp.int32)
    slots = lax.broadcasted_iota(jnp.int32, (ROWS, ROWS), 1)
    pick = ((rank.astype(jnp.int32) - 1 == slots) & (marked > 0)).astype(jnp.float32)
    lane = lax.broadcasted_iota(jnp.int32, (ROWS, D), 1)
    b1 = len_ref[0, 0]
    b2 = b1 + len_ref[0, 1]
    b3 = b2 + len_ref[0, 2]
    start = jnp.where(rows >= b3, b3, jnp.where(rows >= b2, b2, jnp.where(rows >= b1, b1, 0)))
    fields = jnp.where(lane == 0, count, 0.0)
    fields = jnp.where(lane == 1, total_ret, fields)
    fields = jnp.where(lane == 2, rows.astype(jnp.float32), fields)
    fields = jnp.where(lane == 3, start.astype(jnp.float32), fields)
    props[...] = tdot(pick, fields, HIGH)
    pick_low = pick.astype(jnp.bfloat16)
    qc[...] = tdot(pick_low, q_ref[...]).astype(jnp.bfloat16)
    dqc[...] = jnp.zeros_like(dqc)
    dk_ref[...] = jnp.zeros_like(dk_ref)
    w_ref[...] = jnp.zeros_like(w_ref)
    for c in range(KV):
        readout = jnp.concatenate(
            [vhm_ref[h // 5, h % 5 : h % 5 + 1, :] for h in range(c * GROUP, (c + 1) * GROUP)]
            + [jnp.zeros((6, D), jnp.float32)], axis=0,
        )
        high = readout.astype(jnp.bfloat16)
        rest = readout - high.astype(jnp.float32)
        mid = rest.astype(jnp.bfloat16)
        low = (rest - mid.astype(jnp.float32)).astype(jnp.bfloat16)
        values = k_ref[:, (KV + c) * D : (KV + c + 1) * D]
        u_ref[c] = ndot(high, values) + (ndot(mid, values) + ndot(low, values))
    places = (base - 512) + lax.broadcasted_iota(jnp.int32, (1, WIN), 1)

    @pl.loop(0, (n + TILE - 1) // TILE)
    def _(t):
        at = pl.ds(pl.multiple_of(t * TILE, TILE), TILE)
        prop = props[at, :]
        cnt, ret = prop[:, 0:1], prop[:, 1:2]
        row, low = prop[:, 2:3].astype(jnp.int32), prop[:, 3:4].astype(jnp.int32)
        allowed = (places >= low) & (places <= row)
        estimate = jnp.zeros((TILE, 1), jnp.float32)
        for c in range(KV):
            keys = k_ref[:, c * D : (c + 1) * D]
            q = jnp.concatenate(
                [qc[at, (c * GROUP + g) * D : (c * GROUP + g + 1) * D] for g in range(GROUP)], axis=0
            )
            scores = ndot(q, keys) * SCALE
            for g in range(GROUP):
                h = c * GROUP + g
                s = jnp.where(allowed, scores[g * TILE : (g + 1) * TILE, :], NEG)
                e = jnp.exp(s - jnp.max(s, axis=1, keepdims=True))
                p = e / jnp.sum(e, axis=1, keepdims=True)
                probs[h] = p
                low_p = p.astype(jnp.bfloat16).astype(jnp.float32)
                hv = jnp.sum(low_p * u_ref[c, g : g + 1, :], axis=1, keepdims=True)
                heads[h] = hv
                estimate = estimate + hv
        coef = cnt * estimate - ret
        for c in range(KV):
            keys = k_ref[:, c * D : (c + 1) * D]
            q = jnp.concatenate(
                [qc[at, (c * GROUP + g) * D : (c * GROUP + g + 1) * D] for g in range(GROUP)], axis=0
            )
            values = k_ref[:, (KV + c) * D : (KV + c + 1) * D]
            grad_out = jnp.concatenate(
                [
                    (coef * vhm_ref[h // 5, h % 5 : h % 5 + 1, :]).astype(jnp.bfloat16)
                    for h in range(c * GROUP, (c + 1) * GROUP)
                ],
                axis=0,
            )
            grad_probs = ndot(grad_out, values)
            parts = []
            for g in range(GROUP):
                h = c * GROUP + g
                p = probs[h]
                low_p = p.astype(jnp.bfloat16).astype(jnp.float32)
                w_ref[h : h + 1, :] += jnp.sum(low_p * coef, axis=0, keepdims=True)
                grad_p = grad_probs[g * TILE : (g + 1) * TILE, :]
                parts.append((p * (grad_p - coef * heads[h])).astype(jnp.bfloat16))
            gs = jnp.concatenate(parts, axis=0)
            dq = (jnp.dot(gs, keys, preferred_element_type=jnp.float32) * SCALE).astype(jnp.bfloat16)
            for g in range(GROUP):
                h = c * GROUP + g
                dqc[at, h * D : (h + 1) * D] = dq[g * TILE : (g + 1) * TILE, :]
            dk_ref[:, c * D : (c + 1) * D] += tdot(gs, q) * SCALE

    far_ref[...] = dk_ref[: WIN - ROWS, :].astype(jnp.bfloat16)
    near_ref[...] = dk_ref[WIN - ROWS :, :]
    dq_ref[...] = jnp.dot(
        pick_low, dqc[...], preferred_element_type=jnp.float32
    ).astype(jnp.bfloat16)


VMEM = pl.BlockSpec(memory_space=pltpu.VMEM)
SMEM = pl.BlockSpec(memory_space=pltpu.SMEM)


def shape(dims, kind=jnp.bfloat16):
    return jax.ShapeDtypeStruct(dims, kind)


def attention(lengths, positions, returns, queries, keys, vhm):
    return pl.pallas_call(
        attention_kernel,
        out_shape=(
            shape((ROWS, HEADS * D)),
            shape((WIN - ROWS, KV * D)),
            shape((ROWS, KV * D), jnp.float32),
            shape((HEADS, WIN), jnp.float32),
        ),
        in_specs=[SMEM] + [VMEM] * 5,
        out_specs=(VMEM,) * 4,
        scratch_shapes=[
            pltpu.VMEM((ROWS, HEADS * D), jnp.bfloat16),
            pltpu.VMEM((ROWS, HEADS * D), jnp.bfloat16),
            pltpu.VMEM((ROWS, D), jnp.float32),
            pltpu.VMEM((HEADS, TILE, WIN), jnp.float32),
            pltpu.VMEM((HEADS, TILE, 1), jnp.float32),
            pltpu.VMEM((WIN, KV * D), jnp.float32),
            pltpu.VMEM((KV, 16, WIN), jnp.float32),
        ],
        compiler_params=pltpu.CompilerParams(vmem_limit_bytes=48 * 2**20),
    )(lengths, positions, returns, queries, keys, vhm)


MESH = pl.DeviceIdType.MESH
Z, YH, X, YL = 8, 2, 4, 2
Y = YH * YL
SP = X * YL
BACK = 4


class Place:
    def __init__(self):
        fsdp, self.sp = lax.axis_index("fsdp"), lax.axis_index("sp")
        self.core = fsdp % 2
        self.yh = (fsdp // 2) % YH
        self.z = fsdp // 4
        self.x, self.yl = self.sp // YL, self.sp % YL
        self.y = self.yh * YL + self.yl

    def at(self, z=None, yh=None, core=None, x=None, yl=None):
        z = self.z if z is None else z
        yh = self.yh if yh is None else yh
        core = self.core if core is None else core
        x = self.x if x is None else x
        yl = self.yl if yl is None else yl
        return (z * 4 + yh * 2 + core, x * YL + yl)

    def partner(self):
        return self.at(core=1 - self.core)

    def along(self, axis, r):
        if axis == "x":
            x = (self.x + r) % X
            return self.at(x=x), x
        if axis == "z":
            z = (self.z + r) % Z
            return self.at(z=z), z
        y = (self.y + r) % Y
        return self.at(yh=y // YL, yl=y % YL), y

    def slab(self, r):
        return (lax.axis_index("fsdp"), (self.sp + r) % SP)


COUNT = {"x": X, "y": Y, "z": Z}


class Copies:
    def __init__(self, send, recv):
        self.send, self.recv, self.used, self.open = send, recv, 0, []

    def make(self, src, dst, to):
        i = self.used
        self.used += 1
        return pltpu.make_async_remote_copy(
            src_ref=src, dst_ref=dst, send_sem=self.send.at[i], recv_sem=self.recv.at[i],
            device_id=to, device_id_type=MESH,
        )

    def start(self, src, dst, to):
        copy = self.make(src, dst, to)
        copy.start()
        self.open.append(copy)
        return copy

    def close(self):
        for copy in self.open:
            copy.wait_send()


def greet(place):
    barrier = pltpu.get_barrier_semaphore()
    peers = [place.partner()]
    for axis in ("x", "y", "z"):
        peers += [place.along(axis, r)[0] for r in range(1, COUNT[axis])]
    peers += [place.at(x=(place.x + r) % X, yl=1 - place.yl) for r in range(1, X)]
    for peer in peers:
        pl.semaphore_signal(barrier, inc=1, device_id=peer, device_id_type=MESH)
    pl.semaphore_wait(barrier, len(peers))


def gather_kernel(
    t_ref, kv_ref, vhm_ref,
    kwin, vfull, wb, wg, wa, tb,
    tsend, pr, pin, ssem, rsem,
):
    place = Place()
    copies = Copies(ssem, rsem)
    z, yh, x, yl, core, j = place.z, place.yh, place.x, place.yl, place.core, place.sp
    other = 1 - core

    wb[z, yh, x, yl] = kv_ref[:, 0:384]
    wg[z, yh, x, yl] = kv_ref[:, 384:768]
    wa[z, yh, x, yl] = kv_ref[:, 768:1024]
    vfull[j] = vhm_ref[...]
    here = pl.ds(pl.multiple_of(core * ROWS, ROWS), ROWS)
    there = pl.ds(pl.multiple_of(other * ROWS, ROWS), ROWS)
    for b in range(16):
        mine = pl.ds(pl.multiple_of(b * 256 + core * 128, 128), 128)
        theirs = pl.ds(pl.multiple_of(b * 256 + other * 128, 128), 128)
        tb[here, b * 128 : (b + 1) * 128] = t_ref[:, mine]
        tsend[:, b * 128 : (b + 1) * 128] = t_ref[:, theirs]

    greet(place)

    def spread(axis, view):
        return [
            copies.start(view, view, place.along(axis, r)[0]) for r in range(1, COUNT[axis])
        ]

    def arrive(group):
        for copy in group:
            copy.wait_recv()

    b1 = spread("z", wb.at[z, yh, x, yl])
    g1 = spread("z", wg.at[z, yh, x, yl])
    a1 = spread("x", wa.at[z, yh, x, yl])
    v1 = [copies.start(vfull.at[j], vfull.at[j], place.slab(r)) for r in range(1, SP)]
    tswap = copies.start(tsend, tb.at[here, :], place.partner())

    arrive(b1)
    b2 = spread("y", wb.at[:, yh, x, yl])
    arrive(g1)
    g2 = spread("x", wg.at[:, yh, x, yl])
    arrive(a1)
    a2 = spread("y", wa.at[z, yh, :, yl])
    arrive(b2)
    b3 = spread("x", wb.at[:, :, x, :])
    arrive(g2)
    g3 = spread("y", wg.at[:, yh, :, yl])
    arrive(a2)
    a3 = spread("z", wa.at[z])
    arrive([tswap])
    arrive(b3)
    pr[:, 0:384] = jnp.dot(
        tb[...], wb[...].reshape(2048, 384), preferred_element_type=jnp.float32
    )
    arrive(g3)
    pr[:, 384:768] = jnp.dot(
        tb[...], wg[...].reshape(2048, 384), preferred_element_type=jnp.float32
    )
    arrive(a3)
    pr[:, 768:1024] = jnp.dot(
        tb[...], wa[...].reshape(2048, 256), preferred_element_type=jnp.float32
    )
    pswap = copies.start(pr.at[there, :], pin, place.partner())
    arrive([pswap])
    own = slice(WIN - ROWS, WIN)
    kwin[own, :] = (pr[here, :] + pin[...]).astype(jnp.bfloat16)
    moves = []
    for d in range(1, BACK + 1):
        slot = slice((BACK - d) * ROWS, (BACK - d + 1) * ROWS)
        moves.append(copies.make(kwin.at[own, :], kwin.at[slot, :], place.slab(d)))

        @pl.when(j + d < SP)
        def _():
            moves[-1].start()

        @pl.when(j - d < 0)
        def _():
            kwin[slot, :] = jnp.zeros((ROWS, 2 * KV * D), jnp.bfloat16)

    arrive(v1)
    for d in range(1, BACK + 1):

        @pl.when(j - d >= 0)
        def _():
            moves[d - 1].wait_recv()

        @pl.when(j + d < SP)
        def _():
            moves[d - 1].wait_send()

    copies.close()


def gather(tokens, kv_weight, vhm):
    f32 = jnp.float32
    return pl.pallas_call(
        gather_kernel,
        out_shape=(
            shape((WIN, 2 * KV * D)),
            shape((SP, 8, D), f32),
            shape((Z, YH, X, YL, 16, 384)),
            shape((Z, YH, X, YL, 16, 384)),
            shape((Z, YH, X, YL, 16, 256)),
            shape((2 * ROWS, 2048)),
        ),
        in_specs=[VMEM] * 3,
        out_specs=(VMEM,) * 6,
        scratch_shapes=[
            pltpu.VMEM((ROWS, 2048), jnp.bfloat16),
            pltpu.VMEM((2 * ROWS, 1024), f32),
            pltpu.VMEM((ROWS, 1024), f32),
            pltpu.SemaphoreType.DMA((64,)),
            pltpu.SemaphoreType.DMA((64,)),
        ],
        compiler_params=pltpu.CompilerParams(
            collective_id=0, has_side_effects=True, vmem_limit_bytes=48 * 2**20
        ),
    )(tokens, kv_weight, vhm)


def reduce_kernel(
    far_ref, near_ref, w_ref, wb, wg, wa, tb, vfull,
    ig_ref, wgrad_ref,
    readout, rk, rw, gk, gw, gb, pb, pg, pa,
    rb1, rb2, rb3, rg1, rg2, rg3, ra1, ra2, ra3,
    sb1, sb2, sg1, sg2, sa1, sa2, igs, igr, ssem, rsem,
):
    place = Place()
    copies = Copies(ssem, rsem)
    z, yh, x, yl, core, j = place.z, place.yh, place.x, place.yl, place.core, place.sp
    other = 1 - core
    f32 = jnp.float32
    here = pl.ds(pl.multiple_of(core * ROWS, ROWS), ROWS)
    there = pl.ds(pl.multiple_of(other * ROWS, ROWS), ROWS)
    greet(place)

    pairs = []
    for d in range(1, BACK + 1):
        slot = slice((BACK - d) * ROWS, (BACK - d + 1) * ROWS)
        pairs.append(
            (
                copies.make(far_ref.at[slot, :], rk.at[d - 1], place.slab(SP - d)),
                copies.make(w_ref.at[:, slot], rw.at[d - 1], place.slab(SP - d)),
            )
        )

        @pl.when(j - d >= 0)
        def _():
            for copy in pairs[-1]:
                copy.start()

    readout[...] = jnp.zeros_like(readout)
    for h in range(HEADS):
        c = h // GROUP
        readout[h : h + 1, c * D : (c + 1) * D] = vfull[h // 5, h % 5 : h % 5 + 1, :]
    gk[...] = near_ref[...]
    gw[...] = w_ref[:, WIN - ROWS :]
    for d in range(1, BACK + 1):

        @pl.when(j + d < SP)
        def _():
            for copy in pairs[d - 1]:
                copy.wait_recv()
            gk[...] += rk[d - 1].astype(f32)
            gw[...] += rw[d - 1]

    gb[here, 0:512] = gk[...].astype(jnp.bfloat16)
    whi = gw[...].astype(jnp.bfloat16).astype(f32)
    wlo = gw[...] - whi
    stacked = jnp.concatenate([whi, wlo, jnp.zeros((48, ROWS), f32)], axis=0)
    gb[here, 1024:1152] = stacked.T.astype(jnp.bfloat16)
    gb[here, 512:1024] = lax.dot_general(
        gw[...], readout[0:HEADS, :], (((0,), (0,)), ((), ())), precision=HIGH,
        preferred_element_type=f32,
    ).astype(jnp.bfloat16)
    gswap = copies.start(gb.at[here, :], gb.at[here, :], place.partner())
    gswap.wait_recv()

    def rest(axis):
        return range(1, COUNT[axis])

    def add_up(own, slots, n):
        total = own.astype(f32)
        for k in range(n):
            total = total + slots[k].astype(f32)
        return total

    for n in range(Z):
        part = tdot(tb[:, n * 256 : (n + 1) * 256], gb[:, 0:256])
        pb[n] = part.astype(jnp.bfloat16).reshape(YH, X, YL, 16, 256)
    b1 = []
    for r in rest("x"):
        to, at = place.along("x", r)
        b1.append(copies.start(pb.at[:, :, at], rb1.at[r - 1], to))
    for n in range(Z):
        part = tdot(tb[:, n * 256 : (n + 1) * 256], gb[:, 256:512])
        pg[n] = part.astype(jnp.bfloat16).reshape(YH, X, YL, 16, 256)
    g1 = []
    for r in rest("y"):
        to, at = place.along("y", r)
        g1.append(copies.start(pg.at[:, at // YL, :, at % YL], rg1.at[r - 1], to))
    for n in range(Z):
        part = tdot(tb[:, n * 256 : (n + 1) * 256], gb[:, 1024:1152])
        part = part + pltpu.roll(part, 128 - 40, 1)
        pa[n] = part.astype(jnp.bfloat16).reshape(YH, X, YL, 16, 128)
    a1 = []
    for r in rest("z"):
        to, at = place.along("z", r)
        a1.append(copies.start(pa.at[at], ra1.at[r - 1], to))

    for n in range(Z):
        part = ndot(gb[:, 0:384], wb[n].reshape(256, 384))
        part = part + ndot(gb[:, 384:768], wg[n].reshape(256, 384))
        part = part + ndot(gb[:, 768:1024], wa[n].reshape(256, 256))
        igs[:, n * 256 : (n + 1) * 256] = part.astype(jnp.bfloat16)
    iswap = copies.start(igs.at[there, :], igr, place.partner())

    for copy in b1:
        copy.wait_recv()
    sb1[...] = add_up(pb[:, :, x], rb1, X - 1).astype(jnp.bfloat16)
    b2 = []
    for r in rest("y"):
        to, at = place.along("y", r)
        b2.append(copies.start(sb1.at[:, at // YL, at % YL], rb2.at[r - 1], to))
    for copy in g1:
        copy.wait_recv()
    sg1[...] = add_up(pg[:, yh, :, yl], rg1, Y - 1).astype(jnp.bfloat16)
    g2 = []
    for r in rest("x"):
        to, at = place.along("x", r)
        g2.append(copies.start(sg1.at[:, at], rg2.at[r - 1], to))
    for copy in a1:
        copy.wait_recv()
    sa1[...] = add_up(pa[z], ra1, Z - 1).astype(jnp.bfloat16)
    a2 = []
    for r in rest("y"):
        to, at = place.along("y", r)
        a2.append(copies.start(sa1.at[at // YL, :, at % YL], ra2.at[r - 1], to))
    for copy in b2:
        copy.wait_recv()
    sb2[...] = add_up(sb1[:, yh, yl], rb2, Y - 1).astype(jnp.bfloat16)
    b3 = []
    for r in rest("z"):
        to, at = place.along("z", r)
        b3.append(copies.start(sb2.at[at], rb3.at[r - 1], to))
    for copy in g2:
        copy.wait_recv()
    sg2[...] = add_up(sg1[:, x], rg2, X - 1).astype(jnp.bfloat16)
    g3 = []
    for r in rest("z"):
        to, at = place.along("z", r)
        g3.append(copies.start(sg2.at[at], rg3.at[r - 1], to))
    for copy in a2:
        copy.wait_recv()
    sa2[...] = add_up(sa1[yh, :, yl], ra2, Y - 1).astype(jnp.bfloat16)
    a3 = []
    for r in rest("x"):
        to, at = place.along("x", r)
        a3.append(copies.start(sa2.at[at], ra3.at[r - 1], to))

    iswap.wait_recv()
    for b in range(16):
        block = slice(b * 128, (b + 1) * 128)
        mine = pl.ds(pl.multiple_of(b * 256 + core * 128, 128), 128)
        theirs = pl.ds(pl.multiple_of(b * 256 + other * 128, 128), 128)
        ig_ref[:, mine] = igs[here, block]
        ig_ref[:, theirs] = igr[:, block]
    for copy in b3:
        copy.wait_recv()
    wgrad_ref[:, 0:256] = add_up(sb2[z], rb3, Z - 1)
    for copy in g3:
        copy.wait_recv()
    wgrad_ref[:, 256:512] = add_up(sg2[z], rg3, Z - 1)
    for copy in a3:
        copy.wait_recv()
    last = add_up(sa2[x], ra3, X - 1)
    wgrad_ref[:, 512:1024] = jnp.dot(
        last, readout[...], precision=HIGH, preferred_element_type=f32
    )
    for d in range(1, BACK + 1):

        @pl.when(j - d >= 0)
        def _():
            for copy in pairs[d - 1]:
                copy.wait_send()

    copies.close()


def reduce(far, near, w, wb, wg, wa, tb, vfull):
    f32, low = jnp.float32, jnp.bfloat16
    return pl.pallas_call(
        reduce_kernel,
        out_shape=(shape((ROWS, 4096)), shape((16, 1024), f32)),
        in_specs=[VMEM] * 8,
        out_specs=(VMEM, VMEM),
        scratch_shapes=[
            pltpu.VMEM((128, KV * D), f32),
            pltpu.VMEM((BACK, ROWS, KV * D), low),
            pltpu.VMEM((BACK, HEADS, ROWS), f32),
            pltpu.VMEM((ROWS, KV * D), f32),
            pltpu.VMEM((HEADS, ROWS), f32),
            pltpu.VMEM((2 * ROWS, 1152), low),
            pltpu.VMEM((Z, YH, X, YL, 16, 256), low),
            pltpu.VMEM((Z, YH, X, YL, 16, 256), low),
            pltpu.VMEM((Z, YH, X, YL, 16, 128), low),
            pltpu.VMEM((X - 1, Z, YH, YL, 16, 256), low),
            pltpu.VMEM((Y - 1, Z, 16, 256), low),
            pltpu.VMEM((Z - 1, 16, 256), low),
            pltpu.VMEM((Y - 1, Z, X, 16, 256), low),
            pltpu.VMEM((X - 1, Z, 16, 256), low),
            pltpu.VMEM((Z - 1, 16, 256), low),
            pltpu.VMEM((Z - 1, YH, X, YL, 16, 128), low),
            pltpu.VMEM((Y - 1, X, 16, 128), low),
            pltpu.VMEM((X - 1, 16, 128), low),
            pltpu.VMEM((Z, YH, YL, 16, 256), low),
            pltpu.VMEM((Z, 16, 256), low),
            pltpu.VMEM((Z, X, 16, 256), low),
            pltpu.VMEM((Z, 16, 256), low),
            pltpu.VMEM((YH, X, YL, 16, 128), low),
            pltpu.VMEM((X, 16, 128), low),
            pltpu.VMEM((2 * ROWS, 2048), low),
            pltpu.VMEM((ROWS, 2048), low),
            pltpu.SemaphoreType.DMA((64,)),
            pltpu.SemaphoreType.DMA((64,)),
        ],
        compiler_params=pltpu.CompilerParams(
            collective_id=1, has_side_effects=True, vmem_limit_bytes=56 * 2**20
        ),
    )(far, near, w, wb, wg, wa, tb, vfull)


def on_device(tokens, queries, kv_weight, vhm, lengths, positions, returns):
    vhm = jnp.pad(vhm.reshape(HEADS // SP, D), ((0, 8 - HEADS // SP), (0, 0)))
    kwin, vfull, wb, wg, wa, tb = gather(tokens, kv_weight, vhm)
    dq, far, near, w = attention(lengths, positions, returns, queries, kwin, vfull)
    input_grad, weight_grad = reduce(far, near, w, wb, wg, wa, tb, vfull)
    return dq, input_grad, weight_grad


def solution(mesh):
    rows = P(("fsdp", "sp"), None)
    slab = P("fsdp", None)
    return jax.shard_map(
        on_device,
        mesh=mesh,
        in_specs=(rows, rows, rows, P("sp"), slab, slab, slab),
        out_specs=(rows, rows, rows),
        check_vma=False,
    )
```

```python
import math

import jax
import jax.numpy as jnp
from jax import lax
from jax.experimental import pallas as pl
from jax.experimental.pallas import tpu as pltpu
from jax.sharding import PartitionSpec as P

HEADS = 40
KV = 4
GROUP = 10
D = 128
SCALE = 1.0 / math.sqrt(D)
ROWS = 128
WIN = 640
TILE = 48
PADDED = 144
NEG = -1e30
HIGH = lax.Precision.HIGHEST


def tdot(a, b, precision=None):
    return lax.dot_general(
        a, b, (((0,), (0,)), ((), ())), precision=precision, preferred_element_type=jnp.float32
    )


def ndot(a, b):
    return lax.dot_general(a, b, (((1,), (1,)), ((), ())), preferred_element_type=jnp.float32)


def attention_kernel(
    len_hbm, pos_hbm, ret_hbm, q_hbm, k_hbm, v_hbm, vhm_hbm, dq_ref, far_hbm, near_hbm, w_hbm,
    len_ref, pos_ref, ret_ref, q_ref, k_ref, v_ref, vhm_ref,
    qc, dqc, props, probs, heads, dk_ref, u_ref, far_ref, w_ref, sems,
):
    base = lax.axis_index("sp") * ROWS
    moves = [
        pltpu.make_async_copy(src, dst, sems.at[i])
        for i, (src, dst) in enumerate(
            (
                (len_hbm, len_ref), (pos_hbm, pos_ref), (ret_hbm, ret_ref), (q_hbm, q_ref),
                (vhm_hbm, vhm_ref), (v_hbm, v_ref), (k_hbm, k_ref),
            )
        )
    ]
    for move in moves:
        move.start()
    dqc[...] = jnp.zeros_like(dqc)
    dk_ref[...] = jnp.zeros_like(dk_ref)
    w_ref[...] = jnp.zeros_like(w_ref)
    for move in moves[:3]:
        move.wait()
    rows = base + lax.broadcasted_iota(jnp.int32, (ROWS, 1), 0)
    hits = (rows == pos_ref[...]).astype(jnp.float32)
    count = jnp.sum(hits, axis=1, keepdims=True)
    total_ret = jnp.sum(hits * ret_ref[...], axis=1, keepdims=True)
    marked = (count > 0).astype(jnp.float32)
    tri = (
        lax.broadcasted_iota(jnp.int32, (ROWS, ROWS), 1)
        <= lax.broadcasted_iota(jnp.int32, (ROWS, ROWS), 0)
    ).astype(jnp.bfloat16)
    rank = jnp.dot(
        tri, jnp.broadcast_to(marked, (ROWS, D)).astype(jnp.bfloat16),
        preferred_element_type=jnp.float32,
    )
    n = jnp.sum(marked).astype(jnp.int32)
    slots = lax.broadcasted_iota(jnp.int32, (ROWS, ROWS), 1)
    pick = ((rank.astype(jnp.int32) - 1 == slots) & (marked > 0)).astype(jnp.float32)
    lane = lax.broadcasted_iota(jnp.int32, (ROWS, D), 1)
    b1 = len_ref[:, 0:1]
    b2 = b1 + len_ref[:, 1:2]
    b3 = b2 + len_ref[:, 2:3]
    start = jnp.where(rows >= b3, b3, jnp.where(rows >= b2, b2, jnp.where(rows >= b1, b1, 0)))
    fields = jnp.where(lane == 0, count, 0.0)
    fields = jnp.where(lane == 1, total_ret, fields)
    fields = jnp.where(lane == 2, rows.astype(jnp.float32), fields)
    fields = jnp.where(lane == 3, start.astype(jnp.float32), fields)
    props[0:ROWS, :] = tdot(pick, fields, HIGH)
    props[ROWS:, :] = jnp.zeros((PADDED - ROWS, D), jnp.float32)
    pick_low = pick.astype(jnp.bfloat16)
    moves[3].wait()
    qc[0:ROWS, :] = tdot(pick_low, q_ref[...]).astype(jnp.bfloat16)
    qc[ROWS:, :] = jnp.zeros((PADDED - ROWS, HEADS * D), jnp.bfloat16)
    for move in moves[4:]:
        move.wait()
    for c in range(KV):
        readout = jnp.concatenate(
            [vhm_ref[h // 5, h % 5 : h % 5 + 1, :] for h in range(c * GROUP, (c + 1) * GROUP)]
            + [jnp.zeros((6, D), jnp.float32)], axis=0,
        )
        high = readout.astype(jnp.bfloat16)
        rest = readout - high.astype(jnp.float32)
        mid = rest.astype(jnp.bfloat16)
        low = (rest - mid.astype(jnp.float32)).astype(jnp.bfloat16)
        values = v_ref[:, c * D : (c + 1) * D]
        u_ref[c] = ndot(high, values) + (ndot(mid, values) + ndot(low, values))
    places = (base - 512) + lax.broadcasted_iota(jnp.int32, (1, WIN), 1)

    @pl.loop(0, (n + TILE - 1) // TILE)
    def _(t):
        at = pl.ds(pl.multiple_of(t * TILE, 16), TILE)
        prop = props[at, :]
        cnt, ret = prop[:, 0:1], prop[:, 1:2]
        row, low = prop[:, 2:3].astype(jnp.int32), prop[:, 3:4].astype(jnp.int32)
        allowed = (places >= low) & (places <= row)
        estimate = jnp.zeros((TILE, 1), jnp.float32)
        for c in range(KV):
            keys = k_ref[:, c * D : (c + 1) * D]
            q = jnp.concatenate(
                [qc[at, (c * GROUP + g) * D : (c * GROUP + g + 1) * D] for g in range(GROUP)], axis=0
            )
            scores = ndot(q, keys) * SCALE
            for g in range(GROUP):
                h = c * GROUP + g
                s = jnp.where(allowed, scores[g * TILE : (g + 1) * TILE, :], NEG)
                e = jnp.exp(s - jnp.max(s, axis=1, keepdims=True))
                p = e * (1.0 / jnp.sum(e, axis=1, keepdims=True))
                probs[h] = p
                low_p = p.astype(jnp.bfloat16).astype(jnp.float32)
                hv = jnp.sum(low_p * u_ref[c, g : g + 1, :], axis=1, keepdims=True)
                heads[h] = hv
                estimate = estimate + hv
        coef = cnt * estimate - ret
        for c in range(KV):
            keys = k_ref[:, c * D : (c + 1) * D]
            q = jnp.concatenate(
                [qc[at, (c * GROUP + g) * D : (c * GROUP + g + 1) * D] for g in range(GROUP)], axis=0
            )
            values = v_ref[:, c * D : (c + 1) * D]
            grad_out = jnp.concatenate(
                [
                    (coef * vhm_ref[h // 5, h % 5 : h % 5 + 1, :]).astype(jnp.bfloat16)
                    for h in range(c * GROUP, (c + 1) * GROUP)
                ],
                axis=0,
            )
            grad_probs = ndot(grad_out, values)
            parts = []
            for g in range(GROUP):
                h = c * GROUP + g
                p = probs[h]
                low_p = p.astype(jnp.bfloat16).astype(jnp.float32)
                w_ref[h : h + 1, :] += jnp.sum(low_p * coef, axis=0, keepdims=True)
                grad_p = grad_probs[g * TILE : (g + 1) * TILE, :]
                parts.append((p * (grad_p - coef * heads[h])).astype(jnp.bfloat16))
            gs = jnp.concatenate(parts, axis=0)
            dq = (jnp.dot(gs, keys, preferred_element_type=jnp.float32) * SCALE).astype(jnp.bfloat16)
            for g in range(GROUP):
                h = c * GROUP + g
                dqc[at, h * D : (h + 1) * D] = dq[g * TILE : (g + 1) * TILE, :]
            dk_ref[:, c * D : (c + 1) * D] += tdot(gs, q) * SCALE

    far_ref[...] = dk_ref[: WIN - ROWS, :].astype(jnp.bfloat16)
    moves = [
        pltpu.make_async_copy(far_ref, far_hbm, sems.at[0]),
        pltpu.make_async_copy(dk_ref.at[WIN - ROWS :, :], near_hbm, sems.at[1]),
        pltpu.make_async_copy(w_ref, w_hbm, sems.at[2]),
    ]
    for move in moves:
        move.start()
    dq_ref[...] = jnp.dot(
        pick_low, dqc[0:ROWS, :], preferred_element_type=jnp.float32
    ).astype(jnp.bfloat16)
    for move in moves:
        move.wait()


VMEM = pl.BlockSpec(memory_space=pltpu.VMEM)
ANY = pl.BlockSpec(memory_space=pl.ANY)


def shape(dims, kind=jnp.bfloat16):
    return jax.ShapeDtypeStruct(dims, kind)


def attention(lengths, positions, returns, queries, keys, values, vhm):
    return pl.pallas_call(
        attention_kernel,
        out_shape=(
            shape((ROWS, HEADS * D)),
            shape((WIN - ROWS, KV * D)),
            shape((ROWS, KV * D), jnp.float32),
            shape((HEADS, WIN), jnp.float32),
        ),
        in_specs=[ANY] * 7,
        out_specs=(VMEM, ANY, ANY, ANY),
        scratch_shapes=[
            pltpu.VMEM((1, 4), jnp.int32),
            pltpu.VMEM((1, 256), jnp.int32),
            pltpu.VMEM((1, 256), jnp.float32),
            pltpu.VMEM((ROWS, HEADS * D), jnp.bfloat16),
            pltpu.VMEM((WIN, KV * D), jnp.bfloat16),
            pltpu.VMEM((WIN, KV * D), jnp.bfloat16),
            pltpu.VMEM((SP, 8, D), jnp.float32),
            pltpu.VMEM((PADDED, HEADS * D), jnp.bfloat16),
            pltpu.VMEM((PADDED, HEADS * D), jnp.bfloat16),
            pltpu.VMEM((PADDED, D), jnp.float32),
            pltpu.VMEM((HEADS, TILE, WIN), jnp.float32),
            pltpu.VMEM((HEADS, TILE, 1), jnp.float32),
            pltpu.VMEM((WIN, KV * D), jnp.float32),
            pltpu.VMEM((KV, 16, WIN), jnp.float32),
            pltpu.VMEM((WIN - ROWS, KV * D), jnp.bfloat16),
            pltpu.VMEM((HEADS, WIN), jnp.float32),
            pltpu.SemaphoreType.DMA((7,)),
        ],
        compiler_params=pltpu.CompilerParams(vmem_limit_bytes=60 * 2**20),
    )(lengths, positions, returns, queries, keys, values, vhm)


MESH = pl.DeviceIdType.MESH
Z, YH, X, YL = 8, 2, 4, 2
Y = YH * YL
SP = X * YL
BACK = 4


class Place:
    def __init__(self):
        fsdp, self.sp = lax.axis_index("fsdp"), lax.axis_index("sp")
        self.core = fsdp % 2
        self.yh = (fsdp // 2) % YH
        self.z = fsdp // 4
        self.x, self.yl = self.sp // YL, self.sp % YL
        self.y = self.yh * YL + self.yl

    def at(self, z=None, yh=None, core=None, x=None, yl=None):
        z = self.z if z is None else z
        yh = self.yh if yh is None else yh
        core = self.core if core is None else core
        x = self.x if x is None else x
        yl = self.yl if yl is None else yl
        return (z * 4 + yh * 2 + core, x * YL + yl)

    def partner(self):
        return self.at(core=1 - self.core)

    def along(self, axis, r):
        if axis == "x":
            x = (self.x + r) % X
            return self.at(x=x), x
        if axis == "z":
            z = (self.z + r) % Z
            return self.at(z=z), z
        y = (self.y + r) % Y
        return self.at(yh=y // YL, yl=y % YL), y

    def slab(self, r):
        return (lax.axis_index("fsdp"), (self.sp + r) % SP)


COUNT = {"x": X, "y": Y, "z": Z}


class Copies:
    def __init__(self, send, recv):
        self.send, self.recv, self.used, self.open = send, recv, 0, []

    def make(self, src, dst, to):
        i = self.used
        self.used += 1
        return pltpu.make_async_remote_copy(
            src_ref=src, dst_ref=dst, send_sem=self.send.at[i], recv_sem=self.recv.at[i],
            device_id=to, device_id_type=MESH,
        )

    def start(self, src, dst, to):
        copy = self.make(src, dst, to)
        copy.start()
        self.open.append(copy)
        return copy

    def close(self):
        for copy in self.open:
            copy.wait_send()


class Ring4:
    def __init__(self, copies, place, axis, view):
        self.copies, self.view = copies, view
        self.right, _ = place.along(axis, 1)
        self.left, _ = place.along(axis, 3)
        at = getattr(place, axis)
        self.at = [at, (at + 3) % 4, (at + 1) % 4]

    def send(self, at, half, to):
        view = self.view(at, half)
        return self.copies.start(view, view, to)

    def start(self):
        one, two = slice(0, Z // 2), slice(Z // 2, Z)
        self.a = [self.send(self.at[0], h, self.right) for h in (one, two)]
        self.b = [self.send(self.at[0], h, self.left) for h in (two, one)]

    def mid(self):
        self.a[0].wait_recv()
        self.c = self.send(self.at[1], slice(0, Z // 2), self.right)
        self.b[0].wait_recv()
        self.d = self.send(self.at[2], slice(Z // 2, Z), self.left)

    def end(self):
        for copy in (self.a[1], self.b[1], self.c, self.d):
            copy.wait_recv()


class Ring8:
    def __init__(self, copies, place, ref):
        self.copies, self.ref, self.z = copies, ref, place.z
        self.right, _ = place.along("z", 1)
        self.left, _ = place.along("z", Z - 1)
        self.k = 0

    def send(self, at, half, to):
        view = self.ref.at[at, half]
        return self.copies.start(view, view, to)

    def start(self):
        self.a = [self.send(self.z, h, self.right) for h in (0, 1)]
        self.b = [self.send(self.z, h, self.left) for h in (1, 0)]

    def step(self):
        self.k += 1
        last = self.k == Z // 2 - 1
        a, b = self.a, self.b
        self.a, self.b = [], []
        for i, (right, left) in enumerate(((0, 1), (1, 0))):
            a[i].wait_recv()
            if i == 0 or not last:
                self.a.append(self.send((self.z + Z - self.k) % Z, right, self.right))
            b[i].wait_recv()
            if i == 0 or not last:
                self.b.append(self.send((self.z + self.k) % Z, left, self.left))

    def end(self):
        for copy in self.a + self.b:
            copy.wait_recv()


def slot(d):
    return slice((BACK - d) * ROWS, (BACK - d + 1) * ROWS)


class Window:
    def __init__(self, copies, place, ref):
        x, yl = place.x, place.yl
        one, two = place.at(x=(x + 1) % X), place.at(x=(x + 2) % X)
        top, bottom = place.at(yl=1), place.at(yl=0)
        row = [slot(d) for d in range(BACK + 1)]

        def move(src, dst, to, sends, takes):
            return copies.make(ref.at[row[src], :], ref.at[row[dst], :], to), sends, takes

        self.m1 = move(0, 1, top, yl == 0, yl == 1)
        self.m2 = move(0, 2, one, x + 1 < X, x >= 1)
        self.m4 = move(0, 4, two, x + 2 < X, x >= 2)
        self.f1 = move(2, 1, bottom, (yl == 1) & (x >= 1), (yl == 0) & (x >= 1))
        self.f3 = move(2, 3, top, (yl == 0) & (x >= 1), (yl == 1) & (x >= 1))
        self.g3 = move(4, 3, bottom, (yl == 1) & (x >= 2), (yl == 0) & (x >= 2))

    def start(self):
        for copy, sends, _ in (self.m2, self.m4, self.m1):
            pl.when(sends)(copy.start)

    def mid(self):
        copy, _, takes = self.m2
        pl.when(takes)(copy.wait_recv)
        for copy, sends, _ in (self.f1, self.f3):
            pl.when(sends)(copy.start)
        copy, _, takes = self.m4
        pl.when(takes)(copy.wait_recv)
        copy, sends, _ = self.g3
        pl.when(sends)(copy.start)

    def end(self):
        for copy, _, takes in (self.m1, self.f1, self.f3, self.g3):
            pl.when(takes)(copy.wait_recv)
        for copy, sends, _ in (self.m1, self.m2, self.m4, self.f1, self.f3, self.g3):
            pl.when(sends)(copy.wait_send)


def greet(place):
    barrier = pltpu.get_barrier_semaphore()
    peers = [place.partner()]
    for axis in ("x", "y", "z"):
        peers += [place.along(axis, r)[0] for r in range(1, COUNT[axis])]
    peers += [place.at(x=(place.x + r) % X, yl=1 - place.yl) for r in range(1, X)]
    for peer in peers:
        pl.semaphore_signal(barrier, inc=1, device_id=peer, device_id_type=MESH)
    pl.semaphore_wait(barrier, len(peers))


def gather_kernel(
    t_hbm, kv_ref, vhm_ref,
    kwin, vwin, vfull, wb_hbm, wg_hbm, wa_hbm, tb_hbm,
    t_ref, wb, wg, wa, tb, tsend, pk, pv, pink, pinv, ssem, rsem, lsem,
):
    place = Place()
    copies = Copies(ssem, rsem)
    z, yh, x, yl, core, j = place.z, place.yh, place.x, place.yl, place.core, place.sp
    other = 1 - core
    fetch = pltpu.make_async_copy(t_hbm, t_ref, lsem.at[0])
    fetch.start()

    wb[z, yh, x, yl] = kv_ref[:, 0:256]
    wg[z, yh, x, yl] = kv_ref[:, 256:512]
    wa[z, yh, x, yl] = kv_ref[:, 512:1024]
    vfull[j] = jnp.zeros((8, D), jnp.float32)
    vfull[j, 0 : HEADS // SP, :] = vhm_ref[...]
    here = pl.ds(pl.multiple_of(core * ROWS, ROWS), ROWS)
    there = pl.ds(pl.multiple_of(other * ROWS, ROWS), ROWS)

    greet(place)

    def spread(axis, view):
        return [
            copies.start(view, view, place.along(axis, r)[0]) for r in range(1, COUNT[axis])
        ]

    def arrive(group):
        for copy in group:
            copy.wait_recv()

    a1 = spread("x", wa.at[z, yh, x, yl])
    b1 = spread("z", wb.at[z, yh, x, yl])
    g1 = spread("z", wg.at[z, yh, x, yl])
    v1 = [copies.start(vfull.at[j], vfull.at[j], place.slab(r)) for r in range(1, SP)]
    b2 = Ring4(copies, place, "y", lambda y, h: wb.at[h, y // YL, x, y % YL])
    g2 = Ring4(copies, place, "x", lambda x, h: wg.at[h, yh, x, yl])
    b3 = Ring4(copies, place, "x", lambda x, h: wb.at[h, :, x])
    g3 = Ring4(copies, place, "y", lambda y, h: wg.at[h, y // YL, :, y % YL])
    a3 = Ring8(copies, place, wa)

    fetch.wait()
    for b in range(16):
        mine = pl.ds(pl.multiple_of(b * 256 + core * 128, 128), 128)
        theirs = pl.ds(pl.multiple_of(b * 256 + other * 128, 128), 128)
        tb[here, b * 128 : (b + 1) * 128] = t_ref[:, mine]
        tsend[:, b * 128 : (b + 1) * 128] = t_ref[:, theirs]
    tswap = copies.start(tsend, tb.at[here, :], place.partner())

    arrive(a1)
    a2 = spread("y", wa.at[z, yh, :, yl])
    arrive(b1)
    b2.start()
    arrive(g1)
    g2.start()
    arrive(a2)
    a3.start()
    b2.mid()
    g2.mid()
    b2.end()
    b3.start()
    g2.end()
    g3.start()
    for d in range(1, BACK + 1):

        @pl.when(j - d < 0)
        def _():
            kwin[slot(d), :] = jnp.zeros((ROWS, KV * D), jnp.bfloat16)
            vwin[slot(d), :] = jnp.zeros((ROWS, KV * D), jnp.bfloat16)

    a3.step()
    arrive([tswap])
    b3.mid()
    g3.mid()
    a3.step()
    b3.end()
    pk[:, 0:256] = jnp.dot(
        tb[...], wb[...].reshape(2048, 256), preferred_element_type=jnp.float32
    )
    g3.end()
    pk[:, 256:512] = jnp.dot(
        tb[...], wg[...].reshape(2048, 256), preferred_element_type=jnp.float32
    )
    kswap = copies.start(pk.at[there, :], pink, place.partner())
    a3.step()
    keep = [
        pltpu.make_async_copy(src, dst, lsem.at[i])
        for i, (src, dst) in enumerate(((tb, tb_hbm), (wb, wb_hbm), (wg, wg_hbm), (wa, wa_hbm)))
    ]
    for copy in keep[:3]:
        copy.start()
    arrive([kswap])
    kwin[slot(0), :] = (pk[here, :] + pink[...]).astype(jnp.bfloat16)
    keys, values = Window(copies, place, kwin), Window(copies, place, vwin)
    keys.start()
    a3.end()
    keep[3].start()
    pv[...] = jnp.dot(tb[...], wa[...].reshape(2048, 512), preferred_element_type=jnp.float32)
    vswap = copies.start(pv.at[there, :], pinv, place.partner())
    keys.mid()
    arrive([vswap])
    vwin[slot(0), :] = (pv[here, :] + pinv[...]).astype(jnp.bfloat16)
    values.start()
    values.mid()
    arrive(v1)
    keys.end()
    values.end()
    copies.close()
    for copy in keep:
        copy.wait()


def gather(tokens, kv_weight, vhm):
    f32, low = jnp.float32, jnp.bfloat16
    return pl.pallas_call(
        gather_kernel,
        out_shape=(
            shape((WIN, KV * D)),
            shape((WIN, KV * D)),
            shape((SP, 8, D), f32),
            shape((Z, YH, X, YL, 16, 256)),
            shape((Z, YH, X, YL, 16, 256)),
            shape((Z, YH, X, YL, 16, 512)),
            shape((2 * ROWS, 2048)),
        ),
        in_specs=[ANY, VMEM, VMEM],
        out_specs=(VMEM, VMEM, VMEM) + (ANY,) * 4,
        scratch_shapes=[
            pltpu.VMEM((ROWS, 4096), low),
            pltpu.VMEM((Z, YH, X, YL, 16, 256), low),
            pltpu.VMEM((Z, YH, X, YL, 16, 256), low),
            pltpu.VMEM((Z, YH, X, YL, 16, 512), low),
            pltpu.VMEM((2 * ROWS, 2048), low),
            pltpu.VMEM((ROWS, 2048), low),
            pltpu.VMEM((2 * ROWS, 512), f32),
            pltpu.VMEM((2 * ROWS, 512), f32),
            pltpu.VMEM((ROWS, 512), f32),
            pltpu.VMEM((ROWS, 512), f32),
            pltpu.SemaphoreType.DMA((112,)),
            pltpu.SemaphoreType.DMA((112,)),
            pltpu.SemaphoreType.DMA((4,)),
        ],
        compiler_params=pltpu.CompilerParams(
            collective_id=0, has_side_effects=True, vmem_limit_bytes=60 * 2**20
        ),
    )(tokens, kv_weight, vhm)


def reduce_kernel(
    far_ref, near_hbm, w_ref, wb_hbm, wg_hbm, wa_hbm, tb_hbm, vfull_hbm,
    ig_ref, wgrad_ref,
    wb, wg, wa, tb, vfull, readout, rk, rw, gk, gw, gb, pb, pg, pa,
    rb1, rb2, rb3, rg1, rg2, rg3, ra1, ra2, ra3,
    sb1, sb2, sg1, sg2, sa1, sa2, igs, igr, ssem, rsem, lsem,
):
    place = Place()
    copies = Copies(ssem, rsem)
    z, yh, x, yl, core, j = place.z, place.yh, place.x, place.yl, place.core, place.sp
    other = 1 - core
    f32 = jnp.float32
    here = pl.ds(pl.multiple_of(core * ROWS, ROWS), ROWS)
    there = pl.ds(pl.multiple_of(other * ROWS, ROWS), ROWS)
    copied = (
        (near_hbm, gk), (w_ref.at[:, WIN - ROWS :], gw), (vfull_hbm, vfull),
        (tb_hbm, tb), (wb_hbm, wb), (wg_hbm, wg), (wa_hbm, wa),
    )
    fetch = [
        pltpu.make_async_copy(src, dst, lsem.at[i])
        for i, (src, dst) in enumerate(copied)
    ]
    for copy in fetch:
        copy.start()
    greet(place)

    first, second = slice(0, 256), slice(256, 512)
    streams = [[], [], []]
    for d in range(1, BACK + 1):
        rows, to = slot(d), place.slab(SP - d)
        streams[0].append(copies.make(w_ref.at[:, rows], rw.at[d - 1], to))
        for stream, columns in ((streams[1], first), (streams[2], second)):
            stream.append(copies.make(far_ref.at[rows, columns], rk.at[d - 1, :, columns], to))
    for stream in streams:
        for d in range(1, BACK + 1):
            pl.when(j - d >= 0)(stream[d - 1].start)

    def rest(axis):
        return range(1, COUNT[axis])

    def add_up(own, slots, n):
        total = own.astype(f32)
        for k in range(n):
            total = total + slots[k].astype(f32)
        return total

    def swap(columns):
        view = gb.at[here, columns]
        return copies.start(view, view, place.partner())

    def keys_arrive(stream, columns):
        for d in range(1, BACK + 1):

            @pl.when(j + d < SP)
            def _():
                stream[d - 1].wait_recv()
                gk[:, columns] += rk[d - 1, :, columns].astype(f32)

        gb[here, columns] = gk[:, columns].astype(jnp.bfloat16)
        return swap(columns)

    readout[...] = jnp.zeros_like(readout)
    for copy in fetch[:3]:
        copy.wait()
    for h in range(HEADS):
        c = h // GROUP
        readout[h : h + 1, c * D : (c + 1) * D] = vfull[h // 5, h % 5 : h % 5 + 1, :]
    for d in range(1, BACK + 1):

        @pl.when(j + d < SP)
        def _():
            streams[0][d - 1].wait_recv()
            gw[...] += rw[d - 1]

    whi = gw[...].astype(jnp.bfloat16).astype(f32)
    wlo = gw[...] - whi
    stacked = jnp.concatenate([whi, wlo, jnp.zeros((48, ROWS), f32)], axis=0)
    gb[here, 1024:1152] = stacked.T.astype(jnp.bfloat16)
    gb[here, 512:1024] = lax.dot_general(
        gw[...], readout[0:HEADS, :], (((0,), (0,)), ((), ())), precision=HIGH,
        preferred_element_type=f32,
    ).astype(jnp.bfloat16)
    swap_w = swap(slice(512, 1152))
    for copy in fetch[3:]:
        copy.wait()
    swap_w.wait_recv()
    for n in range(Z):
        part = tdot(tb[:, n * 256 : (n + 1) * 256], gb[:, 1024:1152])
        part = part + pltpu.roll(part, 128 - 40, 1)
        pa[n] = part.astype(jnp.bfloat16).reshape(YH, X, YL, 16, 128)
    a1 = []
    for r in rest("z"):
        to, at = place.along("z", r)
        a1.append(copies.start(pa.at[at], ra1.at[r - 1], to))
    swap_b = keys_arrive(streams[1], first)
    swap_b.wait_recv()
    for n in range(Z):
        part = tdot(tb[:, n * 256 : (n + 1) * 256], gb[:, 0:256])
        pb[n] = part.astype(jnp.bfloat16).reshape(YH, X, YL, 16, 256)
    b1 = []
    for r in rest("x"):
        to, at = place.along("x", r)
        b1.append(copies.start(pb.at[:, :, at], rb1.at[r - 1], to))
    swap_g = keys_arrive(streams[2], second)
    swap_g.wait_recv()
    for n in range(Z):
        part = tdot(tb[:, n * 256 : (n + 1) * 256], gb[:, 256:512])
        pg[n] = part.astype(jnp.bfloat16).reshape(YH, X, YL, 16, 256)
    g1 = []
    for r in rest("y"):
        to, at = place.along("y", r)
        g1.append(copies.start(pg.at[:, at // YL, :, at % YL], rg1.at[r - 1], to))

    for n in range(Z):
        part = ndot(gb[:, 0:256], wb[n].reshape(256, 256))
        part = part + ndot(gb[:, 256:512], wg[n].reshape(256, 256))
        part = part + ndot(gb[:, 512:1024], wa[n].reshape(256, 512))
        igs[:, n * 256 : (n + 1) * 256] = part.astype(jnp.bfloat16)
    iswap = copies.start(igs.at[there, :], igr, place.partner())

    for copy in b1:
        copy.wait_recv()
    sb1[...] = add_up(pb[:, :, x], rb1, X - 1).astype(jnp.bfloat16)
    b2 = []
    for r in rest("y"):
        to, at = place.along("y", r)
        b2.append(copies.start(sb1.at[:, at // YL, at % YL], rb2.at[r - 1], to))
    for copy in g1:
        copy.wait_recv()
    sg1[...] = add_up(pg[:, yh, :, yl], rg1, Y - 1).astype(jnp.bfloat16)
    g2 = []
    for r in rest("x"):
        to, at = place.along("x", r)
        g2.append(copies.start(sg1.at[:, at], rg2.at[r - 1], to))
    for copy in a1:
        copy.wait_recv()
    sa1[...] = add_up(pa[z], ra1, Z - 1).astype(jnp.bfloat16)
    a2 = []
    for r in rest("y"):
        to, at = place.along("y", r)
        a2.append(copies.start(sa1.at[at // YL, :, at % YL], ra2.at[r - 1], to))
    for copy in b2:
        copy.wait_recv()
    sb2[...] = add_up(sb1[:, yh, yl], rb2, Y - 1).astype(jnp.bfloat16)
    b3 = []
    for r in rest("z"):
        to, at = place.along("z", r)
        b3.append(copies.start(sb2.at[at], rb3.at[r - 1], to))
    for copy in g2:
        copy.wait_recv()
    sg2[...] = add_up(sg1[:, x], rg2, X - 1).astype(jnp.bfloat16)
    g3 = []
    for r in rest("z"):
        to, at = place.along("z", r)
        g3.append(copies.start(sg2.at[at], rg3.at[r - 1], to))
    for copy in a2:
        copy.wait_recv()
    sa2[...] = add_up(sa1[yh, :, yl], ra2, Y - 1).astype(jnp.bfloat16)
    a3 = []
    for r in rest("x"):
        to, at = place.along("x", r)
        a3.append(copies.start(sa2.at[at], ra3.at[r - 1], to))

    iswap.wait_recv()
    for b in range(16):
        block = slice(b * 128, (b + 1) * 128)
        mine = pl.ds(pl.multiple_of(b * 256 + core * 128, 128), 128)
        theirs = pl.ds(pl.multiple_of(b * 256 + other * 128, 128), 128)
        ig_ref[:, mine] = igs[here, block]
        ig_ref[:, theirs] = igr[:, block]
    for copy in b3:
        copy.wait_recv()
    wgrad_ref[:, 0:256] = add_up(sb2[z], rb3, Z - 1)
    for copy in g3:
        copy.wait_recv()
    wgrad_ref[:, 256:512] = add_up(sg2[z], rg3, Z - 1)
    for copy in a3:
        copy.wait_recv()
    last = add_up(sa2[x], ra3, X - 1)
    wgrad_ref[:, 512:1024] = jnp.dot(
        last, readout[...], precision=HIGH, preferred_element_type=f32
    )
    for d in range(1, BACK + 1):

        @pl.when(j - d >= 0)
        def _():
            for stream in streams:
                stream[d - 1].wait_send()

    copies.close()


def reduce(far, near, w, wb, wg, wa, tb, vfull):
    f32, low = jnp.float32, jnp.bfloat16
    return pl.pallas_call(
        reduce_kernel,
        out_shape=(shape((ROWS, 4096)), shape((16, 1024), f32)),
        in_specs=[ANY] * 8,
        out_specs=(VMEM, VMEM),
        scratch_shapes=[
            pltpu.VMEM((Z, YH, X, YL, 16, 256), low),
            pltpu.VMEM((Z, YH, X, YL, 16, 256), low),
            pltpu.VMEM((Z, YH, X, YL, 16, 512), low),
            pltpu.VMEM((2 * ROWS, 2048), low),
            pltpu.VMEM((SP, 8, D), f32),
            pltpu.VMEM((128, KV * D), f32),
            pltpu.VMEM((BACK, ROWS, KV * D), low),
            pltpu.VMEM((BACK, HEADS, ROWS), f32),
            pltpu.VMEM((ROWS, KV * D), f32),
            pltpu.VMEM((HEADS, ROWS), f32),
            pltpu.VMEM((2 * ROWS, 1152), low),
            pltpu.VMEM((Z, YH, X, YL, 16, 256), low),
            pltpu.VMEM((Z, YH, X, YL, 16, 256), low),
            pltpu.VMEM((Z, YH, X, YL, 16, 128), low),
            pltpu.VMEM((X - 1, Z, YH, YL, 16, 256), low),
            pltpu.VMEM((Y - 1, Z, 16, 256), low),
            pltpu.VMEM((Z - 1, 16, 256), low),
            pltpu.VMEM((Y - 1, Z, X, 16, 256), low),
            pltpu.VMEM((X - 1, Z, 16, 256), low),
            pltpu.VMEM((Z - 1, 16, 256), low),
            pltpu.VMEM((Z - 1, YH, X, YL, 16, 128), low),
            pltpu.VMEM((Y - 1, X, 16, 128), low),
            pltpu.VMEM((X - 1, 16, 128), low),
            pltpu.VMEM((Z, YH, YL, 16, 256), low),
            pltpu.VMEM((Z, 16, 256), low),
            pltpu.VMEM((Z, X, 16, 256), low),
            pltpu.VMEM((Z, 16, 256), low),
            pltpu.VMEM((YH, X, YL, 16, 128), low),
            pltpu.VMEM((X, 16, 128), low),
            pltpu.VMEM((2 * ROWS, 2048), low),
            pltpu.VMEM((ROWS, 2048), low),
            pltpu.SemaphoreType.DMA((64,)),
            pltpu.SemaphoreType.DMA((64,)),
            pltpu.SemaphoreType.DMA((7,)),
        ],
        compiler_params=pltpu.CompilerParams(
            collective_id=1, has_side_effects=True, vmem_limit_bytes=60 * 2**20
        ),
    )(far, near, w, wb, wg, wa, tb, vfull)


def on_device(tokens, queries, kv_weight, vhm, lengths, positions, returns):
    vhm = vhm.reshape(HEADS // SP, D)
    kwin, vwin, vfull, wb, wg, wa, tb = gather(tokens, kv_weight, vhm)
    dq, far, near, w = attention(lengths, positions, returns, queries, kwin, vwin, vfull)
    input_grad, weight_grad = reduce(far, near, w, wb, wg, wa, tb, vfull)
    return dq, input_grad, weight_grad


def solution(mesh):
    rows = P(("fsdp", "sp"), None)
    slab = P("fsdp", None)
    return jax.shard_map(
        on_device,
        mesh=mesh,
        in_specs=(rows, rows, rows, P("sp"), slab, slab, slab),
        out_specs=(rows, rows, rows),
        check_vma=False,
    )
```

```python
import math

import jax
import jax.numpy as jnp
from jax import lax
from jax.experimental import pallas as pl
from jax.experimental.pallas import tpu as pltpu
from jax.sharding import PartitionSpec as P

HEADS = 40
KV = 4
GROUP = 10
D = 128
SCALE = 1.0 / math.sqrt(D)
ROWS = 128
WIN = 640
TILE = 48
PADDED = 144
NEG = -1e30
HIGH = lax.Precision.HIGHEST


def tdot(a, b, precision=None):
    return lax.dot_general(
        a, b, (((0,), (0,)), ((), ())), precision=precision, preferred_element_type=jnp.float32
    )


def ndot(a, b):
    return lax.dot_general(a, b, (((1,), (1,)), ((), ())), preferred_element_type=jnp.float32)


def attention_kernel(
    len_hbm, pos_hbm, ret_hbm, q_hbm, k_hbm, v_hbm, vhm_hbm, dq_ref, far_hbm, near_hbm, w_hbm,
    len_ref, pos_ref, ret_ref, q_ref, k_ref, v_ref, vhm_ref,
    qc, dqc, props, probs, heads, dk_ref, u_ref, far_ref, w_ref, sems,
):
    base = lax.axis_index("sp") * ROWS
    moves = [
        pltpu.make_async_copy(src, dst, sems.at[i])
        for i, (src, dst) in enumerate(
            (
                (len_hbm, len_ref), (pos_hbm, pos_ref), (ret_hbm, ret_ref), (q_hbm, q_ref),
                (vhm_hbm, vhm_ref), (v_hbm, v_ref), (k_hbm, k_ref),
            )
        )
    ]
    for move in moves:
        move.start()
    dqc[...] = jnp.zeros_like(dqc)
    dk_ref[...] = jnp.zeros_like(dk_ref)
    w_ref[...] = jnp.zeros_like(w_ref)
    for move in moves[:3]:
        move.wait()
    rows = base + lax.broadcasted_iota(jnp.int32, (ROWS, 1), 0)
    hits = (rows == pos_ref[...]).astype(jnp.float32)
    count = jnp.sum(hits, axis=1, keepdims=True)
    total_ret = jnp.sum(hits * ret_ref[...], axis=1, keepdims=True)
    marked = (count > 0).astype(jnp.float32)
    tri = (
        lax.broadcasted_iota(jnp.int32, (ROWS, ROWS), 1)
        <= lax.broadcasted_iota(jnp.int32, (ROWS, ROWS), 0)
    ).astype(jnp.bfloat16)
    rank = jnp.dot(
        tri, jnp.broadcast_to(marked, (ROWS, D)).astype(jnp.bfloat16),
        preferred_element_type=jnp.float32,
    )
    n = jnp.sum(marked).astype(jnp.int32)
    slots = lax.broadcasted_iota(jnp.int32, (ROWS, ROWS), 1)
    pick = ((rank.astype(jnp.int32) - 1 == slots) & (marked > 0)).astype(jnp.float32)
    lane = lax.broadcasted_iota(jnp.int32, (ROWS, D), 1)
    b1 = len_ref[:, 0:1]
    b2 = b1 + len_ref[:, 1:2]
    b3 = b2 + len_ref[:, 2:3]
    start = jnp.where(rows >= b3, b3, jnp.where(rows >= b2, b2, jnp.where(rows >= b1, b1, 0)))
    fields = jnp.where(lane == 0, count, 0.0)
    fields = jnp.where(lane == 1, total_ret, fields)
    fields = jnp.where(lane == 2, rows.astype(jnp.float32), fields)
    fields = jnp.where(lane == 3, start.astype(jnp.float32), fields)
    props[0:ROWS, :] = tdot(pick, fields, HIGH)
    props[ROWS:, :] = jnp.zeros((PADDED - ROWS, D), jnp.float32)
    pick_low = pick.astype(jnp.bfloat16)
    moves[3].wait()
    qc[0:ROWS, :] = tdot(pick_low, q_ref[...]).astype(jnp.bfloat16)
    qc[ROWS:, :] = jnp.zeros((PADDED - ROWS, HEADS * D), jnp.bfloat16)
    for move in moves[4:]:
        move.wait()
    for c in range(KV):
        readout = jnp.concatenate(
            [vhm_ref[h // 5, h % 5 : h % 5 + 1, :] for h in range(c * GROUP, (c + 1) * GROUP)]
            + [jnp.zeros((6, D), jnp.float32)], axis=0,
        )
        high = readout.astype(jnp.bfloat16)
        rest = readout - high.astype(jnp.float32)
        mid = rest.astype(jnp.bfloat16)
        low = (rest - mid.astype(jnp.float32)).astype(jnp.bfloat16)
        values = v_ref[:, c * D : (c + 1) * D]
        u_ref[c] = ndot(high, values) + (ndot(mid, values) + ndot(low, values))
    places = (base - 512) + lax.broadcasted_iota(jnp.int32, (1, WIN), 1)

    @pl.loop(0, (n + TILE - 1) // TILE)
    def _(t):
        at = pl.ds(pl.multiple_of(t * TILE, 16), TILE)
        prop = props[at, :]
        cnt, ret = prop[:, 0:1], prop[:, 1:2]
        row, low = prop[:, 2:3].astype(jnp.int32), prop[:, 3:4].astype(jnp.int32)
        allowed = (places >= low) & (places <= row)
        estimate = jnp.zeros((TILE, 1), jnp.float32)
        for c in range(KV):
            keys = k_ref[:, c * D : (c + 1) * D]
            q = jnp.concatenate(
                [qc[at, (c * GROUP + g) * D : (c * GROUP + g + 1) * D] for g in range(GROUP)], axis=0
            )
            scores = ndot(q, keys) * SCALE
            for g in range(GROUP):
                h = c * GROUP + g
                s = jnp.where(allowed, scores[g * TILE : (g + 1) * TILE, :], NEG)
                e = jnp.exp(s - jnp.max(s, axis=1, keepdims=True))
                p = e * (1.0 / jnp.sum(e, axis=1, keepdims=True))
                probs[h] = p
                low_p = p.astype(jnp.bfloat16).astype(jnp.float32)
                hv = jnp.sum(low_p * u_ref[c, g : g + 1, :], axis=1, keepdims=True)
                heads[h] = hv
                estimate = estimate + hv
        coef = cnt * estimate - ret
        for c in range(KV):
            keys = k_ref[:, c * D : (c + 1) * D]
            q = jnp.concatenate(
                [qc[at, (c * GROUP + g) * D : (c * GROUP + g + 1) * D] for g in range(GROUP)], axis=0
            )
            values = v_ref[:, c * D : (c + 1) * D]
            grad_out = jnp.concatenate(
                [
                    (coef * vhm_ref[h // 5, h % 5 : h % 5 + 1, :]).astype(jnp.bfloat16)
                    for h in range(c * GROUP, (c + 1) * GROUP)
                ],
                axis=0,
            )
            grad_probs = ndot(grad_out, values)
            parts = []
            for g in range(GROUP):
                h = c * GROUP + g
                p = probs[h]
                low_p = p.astype(jnp.bfloat16).astype(jnp.float32)
                w_ref[h : h + 1, :] += jnp.sum(low_p * coef, axis=0, keepdims=True)
                grad_p = grad_probs[g * TILE : (g + 1) * TILE, :]
                parts.append((p * (grad_p - coef * heads[h])).astype(jnp.bfloat16))
            gs = jnp.concatenate(parts, axis=0)
            dq = (jnp.dot(gs, keys, preferred_element_type=jnp.float32) * SCALE).astype(jnp.bfloat16)
            for g in range(GROUP):
                h = c * GROUP + g
                dqc[at, h * D : (h + 1) * D] = dq[g * TILE : (g + 1) * TILE, :]
            dk_ref[:, c * D : (c + 1) * D] += tdot(gs, q) * SCALE

    far_ref[...] = dk_ref[: WIN - ROWS, :].astype(jnp.bfloat16)
    moves = [
        pltpu.make_async_copy(far_ref, far_hbm, sems.at[0]),
        pltpu.make_async_copy(dk_ref.at[WIN - ROWS :, :], near_hbm, sems.at[1]),
        pltpu.make_async_copy(w_ref, w_hbm, sems.at[2]),
    ]
    for move in moves:
        move.start()
    dq_ref[...] = jnp.dot(
        pick_low, dqc[0:ROWS, :], preferred_element_type=jnp.float32
    ).astype(jnp.bfloat16)
    for move in moves:
        move.wait()


VMEM = pl.BlockSpec(memory_space=pltpu.VMEM)
ANY = pl.BlockSpec(memory_space=pl.ANY)


def shape(dims, kind=jnp.bfloat16):
    return jax.ShapeDtypeStruct(dims, kind)


def attention(lengths, positions, returns, queries, keys, values, vhm):
    return pl.pallas_call(
        attention_kernel,
        out_shape=(
            shape((ROWS, HEADS * D)),
            shape((WIN - ROWS, KV * D)),
            shape((ROWS, KV * D), jnp.float32),
            shape((HEADS, WIN), jnp.float32),
        ),
        in_specs=[ANY] * 7,
        out_specs=(VMEM, ANY, ANY, ANY),
        scratch_shapes=[
            pltpu.VMEM((1, 4), jnp.int32),
            pltpu.VMEM((1, 256), jnp.int32),
            pltpu.VMEM((1, 256), jnp.float32),
            pltpu.VMEM((ROWS, HEADS * D), jnp.bfloat16),
            pltpu.VMEM((WIN, KV * D), jnp.bfloat16),
            pltpu.VMEM((WIN, KV * D), jnp.bfloat16),
            pltpu.VMEM((SP, 8, D), jnp.float32),
            pltpu.VMEM((PADDED, HEADS * D), jnp.bfloat16),
            pltpu.VMEM((PADDED, HEADS * D), jnp.bfloat16),
            pltpu.VMEM((PADDED, D), jnp.float32),
            pltpu.VMEM((HEADS, TILE, WIN), jnp.float32),
            pltpu.VMEM((HEADS, TILE, 1), jnp.float32),
            pltpu.VMEM((WIN, KV * D), jnp.float32),
            pltpu.VMEM((KV, 16, WIN), jnp.float32),
            pltpu.VMEM((WIN - ROWS, KV * D), jnp.bfloat16),
            pltpu.VMEM((HEADS, WIN), jnp.float32),
            pltpu.SemaphoreType.DMA((7,)),
        ],
        compiler_params=pltpu.CompilerParams(vmem_limit_bytes=60 * 2**20),
    )(lengths, positions, returns, queries, keys, values, vhm)


MESH = pl.DeviceIdType.MESH
Z, YH, X, YL = 8, 2, 4, 2
Y = YH * YL
SP = X * YL
BACK = 4


class Place:
    def __init__(self):
        fsdp, self.sp = lax.axis_index("fsdp"), lax.axis_index("sp")
        self.core = fsdp % 2
        self.yh = (fsdp // 2) % YH
        self.z = fsdp // 4
        self.x, self.yl = self.sp // YL, self.sp % YL
        self.y = self.yh * YL + self.yl

    def at(self, z=None, yh=None, core=None, x=None, yl=None):
        z = self.z if z is None else z
        yh = self.yh if yh is None else yh
        core = self.core if core is None else core
        x = self.x if x is None else x
        yl = self.yl if yl is None else yl
        return (z * 4 + yh * 2 + core, x * YL + yl)

    def partner(self):
        return self.at(core=1 - self.core)

    def along(self, axis, r):
        if axis == "x":
            x = (self.x + r) % X
            return self.at(x=x), x
        if axis == "z":
            z = (self.z + r) % Z
            return self.at(z=z), z
        y = (self.y + r) % Y
        return self.at(yh=y // YL, yl=y % YL), y

    def slab(self, r):
        return (lax.axis_index("fsdp"), (self.sp + r) % SP)


COUNT = {"x": X, "y": Y, "z": Z}


class Copies:
    def __init__(self, send, recv):
        self.send, self.recv, self.used, self.open = send, recv, 0, []

    def make(self, src, dst, to):
        i = self.used
        self.used += 1
        return pltpu.make_async_remote_copy(
            src_ref=src, dst_ref=dst, send_sem=self.send.at[i], recv_sem=self.recv.at[i],
            device_id=to, device_id_type=MESH,
        )

    def start(self, src, dst, to):
        copy = self.make(src, dst, to)
        copy.start()
        self.open.append(copy)
        return copy

    def close(self):
        for copy in self.open:
            copy.wait_send()


class Ring4:
    def __init__(self, copies, place, axis, view):
        self.copies, self.view = copies, view
        self.right, _ = place.along(axis, 1)
        self.left, _ = place.along(axis, 3)
        at = getattr(place, axis)
        self.at = [at, (at + 3) % 4, (at + 1) % 4]

    def send(self, at, half, to):
        view = self.view(at, half)
        return self.copies.start(view, view, to)

    def start(self):
        one, two = slice(0, Z // 2), slice(Z // 2, Z)
        self.a = [self.send(self.at[0], h, self.right) for h in (one, two)]
        self.b = [self.send(self.at[0], h, self.left) for h in (two, one)]

    def mid(self):
        self.a[0].wait_recv()
        self.c = self.send(self.at[1], slice(0, Z // 2), self.right)
        self.b[0].wait_recv()
        self.d = self.send(self.at[2], slice(Z // 2, Z), self.left)

    def end(self):
        for copy in (self.a[1], self.b[1], self.c, self.d):
            copy.wait_recv()


class Ring8:
    def __init__(self, copies, place, ref):
        self.copies, self.ref, self.z = copies, ref, place.z
        self.right, _ = place.along("z", 1)
        self.left, _ = place.along("z", Z - 1)
        self.k = 0

    def send(self, at, half, to):
        view = self.ref.at[at, half]
        return self.copies.start(view, view, to)

    def start(self):
        self.a = [self.send(self.z, h, self.right) for h in (0, 1)]
        self.b = [self.send(self.z, h, self.left) for h in (1, 0)]

    def step(self):
        self.k += 1
        last = self.k == Z // 2 - 1
        a, b = self.a, self.b
        self.a, self.b = [], []
        for i, (right, left) in enumerate(((0, 1), (1, 0))):
            a[i].wait_recv()
            if i == 0 or not last:
                self.a.append(self.send((self.z + Z - self.k) % Z, right, self.right))
            b[i].wait_recv()
            if i == 0 or not last:
                self.b.append(self.send((self.z + self.k) % Z, left, self.left))

    def end(self):
        for copy in self.a + self.b:
            copy.wait_recv()


def slot(d):
    return slice((BACK - d) * ROWS, (BACK - d + 1) * ROWS)


class Window:
    def __init__(self, copies, place, ref):
        x, yl = place.x, place.yl
        one, two = place.at(x=(x + 1) % X), place.at(x=(x + 2) % X)
        top, bottom = place.at(yl=1), place.at(yl=0)
        row = [slot(d) for d in range(BACK + 1)]

        def move(src, dst, to, sends, takes):
            return copies.make(ref.at[row[src], :], ref.at[row[dst], :], to), sends, takes

        self.m1 = move(0, 1, top, yl == 0, yl == 1)
        self.m2 = move(0, 2, one, x + 1 < X, x >= 1)
        self.m4 = move(0, 4, two, x + 2 < X, x >= 2)
        self.f1 = move(2, 1, bottom, (yl == 1) & (x >= 1), (yl == 0) & (x >= 1))
        self.f3 = move(2, 3, top, (yl == 0) & (x >= 1), (yl == 1) & (x >= 1))
        self.g3 = move(4, 3, bottom, (yl == 1) & (x >= 2), (yl == 0) & (x >= 2))

    def start(self):
        for copy, sends, _ in (self.m2, self.m4, self.m1):
            pl.when(sends)(copy.start)

    def mid(self):
        copy, _, takes = self.m2
        pl.when(takes)(copy.wait_recv)
        for copy, sends, _ in (self.f1, self.f3):
            pl.when(sends)(copy.start)
        copy, _, takes = self.m4
        pl.when(takes)(copy.wait_recv)
        copy, sends, _ = self.g3
        pl.when(sends)(copy.start)

    def end(self):
        for copy, _, takes in (self.m1, self.f1, self.f3, self.g3):
            pl.when(takes)(copy.wait_recv)
        for copy, sends, _ in (self.m1, self.m2, self.m4, self.f1, self.f3, self.g3):
            pl.when(sends)(copy.wait_send)


def greet(place):
    barrier = pltpu.get_barrier_semaphore()
    peers = [place.partner()]
    for axis in ("x", "y", "z"):
        peers += [place.along(axis, r)[0] for r in range(1, COUNT[axis])]
    peers += [place.at(x=(place.x + r) % X, yl=1 - place.yl) for r in range(1, X)]
    for peer in peers:
        pl.semaphore_signal(barrier, inc=1, device_id=peer, device_id_type=MESH)
    pl.semaphore_wait(barrier, len(peers))


class Return:
    def __init__(self, copies, place, out, have, by_y, by_x, sum2, sum4, total, columns):
        x, yl = place.x, place.yl
        self.x, self.yl, self.have = x, yl, have
        self.total = total.at[:, columns]
        self.ya, self.yb = by_y.at[0, :, columns], by_y.at[1, :, columns]
        self.xa, self.xb = by_x.at[0, :, columns], by_x.at[1, :, columns]
        self.sum2, self.sum4 = sum2.at[:, columns], sum4.at[:, columns]
        across = place.at(yl=1 - yl)
        one, two = place.at(x=(x + X - 1) % X), place.at(x=(x + X - 2) % X)
        self.top, self.bottom = yl == 1, yl == 0
        self.a = copies.make(out(1), self.ya, across)
        self.b = copies.make(out(3), self.yb, across)
        self.c = copies.make(self.sum2, self.xa, one)
        self.d = copies.make(self.sum4, self.xb, two)
        self.a_sends = self.top | (x >= 1)
        self.b_sends = (self.top & (x >= 1)) | (self.bottom & (x >= 2))
        self.b_takes = (self.bottom & (x >= 1)) | (self.top & (x >= 2))
        self.a_takes = self.bottom | (x >= 1)

    def start(self):
        pl.when(self.a_sends)(self.a.start)
        pl.when(self.b_sends)(self.b.start)

    def add(self, condition, to, what):
        @pl.when(condition)
        def _():
            to[...] = (to[...].astype(jnp.float32) + what[...].astype(jnp.float32)).astype(to.dtype)

    def mid(self):
        x = self.x
        self.sum2[...] = self.have(2)[...]
        self.sum4[...] = self.have(4)[...]
        pl.when(self.a_takes)(self.a.wait_recv)
        pl.when(self.b_takes)(self.b.wait_recv)
        self.add(self.bottom & (x >= 1), self.sum2, self.yb)
        self.add(self.top & (x >= 1), self.sum2, self.ya)
        self.add(self.top & (x >= 2), self.sum4, self.yb)
        self.add(self.bottom, self.total, self.ya)
        pl.when(x >= 1)(self.c.start)
        pl.when(x >= 2)(self.d.start)

    def end(self):
        x = self.x
        pl.when(x + 1 < X)(self.c.wait_recv)
        self.add(x + 1 < X, self.total, self.xa)
        pl.when(x + 2 < X)(self.d.wait_recv)
        self.add(x + 2 < X, self.total, self.xb)

    def close(self):
        x = self.x
        pl.when(self.a_sends)(self.a.wait_send)
        pl.when(self.b_sends)(self.b.wait_send)
        pl.when(x >= 1)(self.c.wait_send)
        pl.when(x >= 2)(self.d.wait_send)


def gather_kernel(
    t_hbm, kv_ref, vhm_ref,
    kwin, vwin, vfull, wb_hbm, wg_hbm, wa_hbm, wd_hbm, tb_hbm,
    t_ref, wb, wg, wa, wd, tb, tsend, pk, pv, pink, pinv, ssem, rsem, lsem,
):
    place = Place()
    copies = Copies(ssem, rsem)
    z, yh, x, yl, core, j = place.z, place.yh, place.x, place.yl, place.core, place.sp
    other = 1 - core
    fetch = pltpu.make_async_copy(t_hbm, t_ref, lsem.at[0])
    fetch.start()

    wb[z, yh, x, yl] = kv_ref[:, 0:256]
    wg[z, yh, x, yl] = kv_ref[:, 256:512]
    wa[z, yh, x, yl] = kv_ref[:, 512:896]
    wd[z, yh, x, yl] = kv_ref[:, 896:1024]
    vfull[j] = jnp.zeros((8, D), jnp.float32)
    vfull[j, 0 : HEADS // SP, :] = vhm_ref[...]
    here = pl.ds(pl.multiple_of(core * ROWS, ROWS), ROWS)
    there = pl.ds(pl.multiple_of(other * ROWS, ROWS), ROWS)

    greet(place)

    def spread(axis, view):
        return [
            copies.start(view, view, place.along(axis, r)[0]) for r in range(1, COUNT[axis])
        ]

    def arrive(group):
        for copy in group:
            copy.wait_recv()

    a1 = spread("x", wa.at[z, yh, x, yl])
    b1 = spread("z", wb.at[z, yh, x, yl])
    g1 = spread("z", wg.at[z, yh, x, yl])
    d1 = spread("z", wd.at[z, yh, x, yl])
    v1 = [copies.start(vfull.at[j], vfull.at[j], place.slab(r)) for r in range(1, SP)]
    b3 = Ring4(copies, place, "x", lambda x, h: wb.at[h, :, x])
    g3 = Ring4(copies, place, "y", lambda y, h: wg.at[h, y // YL, :, y % YL])
    d3 = Ring4(copies, place, "y", lambda y, h: wd.at[h, y // YL, :, y % YL])
    a3 = Ring8(copies, place, wa)

    fetch.wait()
    for b in range(16):
        mine = pl.ds(pl.multiple_of(b * 256 + core * 128, 128), 128)
        theirs = pl.ds(pl.multiple_of(b * 256 + other * 128, 128), 128)
        tb[here, b * 128 : (b + 1) * 128] = t_ref[:, mine]
        tsend[:, b * 128 : (b + 1) * 128] = t_ref[:, theirs]
    tswap = copies.start(tsend, tb.at[here, :], place.partner())

    arrive(a1)
    a2 = spread("y", wa.at[z, yh, :, yl])
    arrive(b1)
    b2 = spread("y", wb.at[:, yh, x, yl])
    arrive(g1)
    g2 = spread("x", wg.at[:, yh, x, yl])
    arrive(a2)
    a3.start()
    arrive(d1)
    d2 = spread("x", wd.at[:, yh, x, yl])
    arrive(b2)
    b3.start()
    arrive(g2)
    g3.start()
    arrive(d2)
    for d in range(1, BACK + 1):

        @pl.when(j - d < 0)
        def _():
            kwin[slot(d), :] = jnp.zeros((ROWS, KV * D), jnp.bfloat16)
            vwin[slot(d), :] = jnp.zeros((ROWS, KV * D), jnp.bfloat16)

    a3.step()
    arrive([tswap])
    b3.mid()
    g3.mid()
    d3.start()
    a3.step()
    b3.end()
    pk[:, 0:256] = jnp.dot(
        tb[...], wb[...].reshape(2048, 256), preferred_element_type=jnp.float32
    )
    g3.end()
    pk[:, 256:512] = jnp.dot(
        tb[...], wg[...].reshape(2048, 256), preferred_element_type=jnp.float32
    )
    kswap = copies.start(pk.at[there, :], pink, place.partner())
    d3.mid()
    a3.step()
    keep = [
        pltpu.make_async_copy(src, dst, lsem.at[i])
        for i, (src, dst) in enumerate(((tb, tb_hbm), (wb, wb_hbm), (wg, wg_hbm), (wa, wa_hbm), (wd, wd_hbm)))
    ]
    for copy in keep[:3]:
        copy.start()
    arrive([kswap])
    kwin[slot(0), :] = (pk[here, :] + pink[...]).astype(jnp.bfloat16)
    keys, values = Window(copies, place, kwin), Window(copies, place, vwin)
    keys.start()
    d3.end()
    keep[4].start()
    pv[:, 384:512] = jnp.dot(
        tb[...], wd[...].reshape(2048, 128), preferred_element_type=jnp.float32
    )
    a3.end()
    keep[3].start()
    pv[:, 0:384] = jnp.dot(
        tb[...], wa[...].reshape(2048, 384), preferred_element_type=jnp.float32
    )
    vswap = copies.start(pv.at[there, :], pinv, place.partner())
    keys.mid()
    arrive([vswap])
    vwin[slot(0), :] = (pv[here, :] + pinv[...]).astype(jnp.bfloat16)
    values.start()
    values.mid()
    arrive(v1)
    keys.end()
    values.end()
    copies.close()
    for copy in keep:
        copy.wait()


def gather(tokens, kv_weight, vhm):
    f32, low = jnp.float32, jnp.bfloat16
    return pl.pallas_call(
        gather_kernel,
        out_shape=(
            shape((WIN, KV * D)),
            shape((WIN, KV * D)),
            shape((SP, 8, D), f32),
            shape((Z, YH, X, YL, 16, 256)),
            shape((Z, YH, X, YL, 16, 256)),
            shape((Z, YH, X, YL, 16, 384)),
            shape((Z, YH, X, YL, 16, 128)),
            shape((2 * ROWS, 2048)),
        ),
        in_specs=[ANY, VMEM, VMEM],
        out_specs=(VMEM, VMEM, VMEM) + (ANY,) * 5,
        scratch_shapes=[
            pltpu.VMEM((ROWS, 4096), low),
            pltpu.VMEM((Z, YH, X, YL, 16, 256), low),
            pltpu.VMEM((Z, YH, X, YL, 16, 256), low),
            pltpu.VMEM((Z, YH, X, YL, 16, 384), low),
            pltpu.VMEM((Z, YH, X, YL, 16, 128), low),
            pltpu.VMEM((2 * ROWS, 2048), low),
            pltpu.VMEM((ROWS, 2048), low),
            pltpu.VMEM((2 * ROWS, 512), f32),
            pltpu.VMEM((2 * ROWS, 512), f32),
            pltpu.VMEM((ROWS, 512), f32),
            pltpu.VMEM((ROWS, 512), f32),
            pltpu.SemaphoreType.DMA((112,)),
            pltpu.SemaphoreType.DMA((112,)),
            pltpu.SemaphoreType.DMA((5,)),
        ],
        compiler_params=pltpu.CompilerParams(
            collective_id=0, has_side_effects=True, vmem_limit_bytes=60 * 2**20
        ),
    )(tokens, kv_weight, vhm)


def reduce_kernel(
    far_ref, near_hbm, w_ref, wb_hbm, wg_hbm, wa_hbm, wd_hbm, tb_hbm, vfull_hbm,
    ig_ref, wgrad_ref,
    wb, wg, wa, wd, tb, vfull, far, wfar, readout, ky, kx, k2, k4, wy, wx, w2, w4, gk, gw, gb, pb, pg, pa,
    rb1, rb2, rb3, rg1, rg2, rg3, ra1, ra2, ra3,
    sb1, sb2, sg1, sg2, sa1, sa2, igs, igr, ssem, rsem, lsem,
):
    place = Place()
    copies = Copies(ssem, rsem)
    z, yh, x, yl, core, j = place.z, place.yh, place.x, place.yl, place.core, place.sp
    other = 1 - core
    f32 = jnp.float32
    here = pl.ds(pl.multiple_of(core * ROWS, ROWS), ROWS)
    there = pl.ds(pl.multiple_of(other * ROWS, ROWS), ROWS)
    copied = (
        (near_hbm, gk), (w_ref.at[:, WIN - ROWS :], gw), (vfull_hbm, vfull),
        (far_ref, far), (w_ref, wfar),
        (tb_hbm, tb), (wb_hbm, wb), (wg_hbm, wg), (wa_hbm, wa), (wd_hbm, wd),
    )
    fetch = [
        pltpu.make_async_copy(src, dst, lsem.at[i])
        for i, (src, dst) in enumerate(copied)
    ]
    for copy in fetch:
        copy.start()
    greet(place)

    first, second = slice(0, 256), slice(256, 512)
    everything = slice(None)
    streams = [
        Return(
            copies, place,
            lambda d: w_ref.at[:, slot(d)], lambda d: wfar.at[:, slot(d)], wy, wx, w2, w4, gw,
            everything,
        )
    ]
    for columns in (first, second):
        streams.append(
            Return(
                copies, place,
                lambda d, columns=columns: far_ref.at[slot(d), columns],
                lambda d, columns=columns: far.at[slot(d), columns],
                ky, kx, k2, k4, gk, columns,
            )
        )
    for stream in streams:
        stream.start()

    def rest(axis):
        return range(1, COUNT[axis])

    def add_up(own, slots, n):
        total = own.astype(f32)
        for k in range(n):
            total = total + slots[k].astype(f32)
        return total

    def swap(columns):
        view = gb.at[here, columns]
        return copies.start(view, view, place.partner())

    def keys_arrive(stream, columns):
        stream.end()
        gb[here, columns] = gk[:, columns].astype(jnp.bfloat16)
        return swap(columns)

    readout[...] = jnp.zeros_like(readout)
    for copy in fetch[2:3]:
        copy.wait()
    for h in range(HEADS):
        c = h // GROUP
        readout[h : h + 1, c * D : (c + 1) * D] = vfull[h // 5, h % 5 : h % 5 + 1, :]
    for copy in fetch[0:2] + fetch[3:5]:
        copy.wait()
    for stream in streams:
        stream.mid()
    streams[0].end()
    whi = gw[...].astype(jnp.bfloat16).astype(f32)
    wlo = gw[...] - whi
    stacked = jnp.concatenate([whi, wlo, jnp.zeros((48, ROWS), f32)], axis=0)
    gb[here, 1024:1152] = stacked.T.astype(jnp.bfloat16)
    gb[here, 512:1024] = lax.dot_general(
        gw[...], readout[0:HEADS, :], (((0,), (0,)), ((), ())), precision=HIGH,
        preferred_element_type=f32,
    ).astype(jnp.bfloat16)
    swap_w = swap(slice(512, 1152))
    for copy in fetch[5:]:
        copy.wait()
    swap_w.wait_recv()
    for n in range(Z):
        part = tdot(tb[:, n * 256 : (n + 1) * 256], gb[:, 1024:1152])
        part = part + pltpu.roll(part, 128 - 40, 1)
        pa[n] = part.astype(jnp.bfloat16).reshape(YH, X, YL, 16, 128)
    a1 = []
    for r in rest("z"):
        to, at = place.along("z", r)
        a1.append(copies.start(pa.at[at], ra1.at[r - 1], to))
    swap_b = keys_arrive(streams[1], first)
    swap_b.wait_recv()
    for n in range(Z):
        part = tdot(tb[:, n * 256 : (n + 1) * 256], gb[:, 0:256])
        pb[n] = part.astype(jnp.bfloat16).reshape(YH, X, YL, 16, 256)
    b1 = []
    for r in rest("x"):
        to, at = place.along("x", r)
        b1.append(copies.start(pb.at[:, :, at], rb1.at[r - 1], to))
    swap_g = keys_arrive(streams[2], second)
    swap_g.wait_recv()
    for n in range(Z):
        part = tdot(tb[:, n * 256 : (n + 1) * 256], gb[:, 256:512])
        pg[n] = part.astype(jnp.bfloat16).reshape(YH, X, YL, 16, 256)
    g1 = []
    for r in rest("y"):
        to, at = place.along("y", r)
        g1.append(copies.start(pg.at[:, at // YL, :, at % YL], rg1.at[r - 1], to))

    for n in range(Z):
        part = ndot(gb[:, 0:256], wb[n].reshape(256, 256))
        part = part + ndot(gb[:, 256:512], wg[n].reshape(256, 256))
        part = part + ndot(gb[:, 512:896], wa[n].reshape(256, 384))
        part = part + ndot(gb[:, 896:1024], wd[n].reshape(256, 128))
        igs[:, n * 256 : (n + 1) * 256] = part.astype(jnp.bfloat16)
    iswap = copies.start(igs.at[there, :], igr, place.partner())

    for copy in b1:
        copy.wait_recv()
    sb1[...] = add_up(pb[:, :, x], rb1, X - 1).astype(jnp.bfloat16)
    b2 = []
    for r in rest("y"):
        to, at = place.along("y", r)
        b2.append(copies.start(sb1.at[:, at // YL, at % YL], rb2.at[r - 1], to))
    for copy in g1:
        copy.wait_recv()
    sg1[...] = add_up(pg[:, yh, :, yl], rg1, Y - 1).astype(jnp.bfloat16)
    g2 = []
    for r in rest("x"):
        to, at = place.along("x", r)
        g2.append(copies.start(sg1.at[:, at], rg2.at[r - 1], to))
    for copy in a1:
        copy.wait_recv()
    sa1[...] = add_up(pa[z], ra1, Z - 1).astype(jnp.bfloat16)
    a2 = []
    for r in rest("y"):
        to, at = place.along("y", r)
        a2.append(copies.start(sa1.at[at // YL, :, at % YL], ra2.at[r - 1], to))
    for copy in b2:
        copy.wait_recv()
    sb2[...] = add_up(sb1[:, yh, yl], rb2, Y - 1).astype(jnp.bfloat16)
    b3 = []
    for r in rest("z"):
        to, at = place.along("z", r)
        b3.append(copies.start(sb2.at[at], rb3.at[r - 1], to))
    for copy in g2:
        copy.wait_recv()
    sg2[...] = add_up(sg1[:, x], rg2, X - 1).astype(jnp.bfloat16)
    g3 = []
    for r in rest("z"):
        to, at = place.along("z", r)
        g3.append(copies.start(sg2.at[at], rg3.at[r - 1], to))
    for copy in a2:
        copy.wait_recv()
    sa2[...] = add_up(sa1[yh, :, yl], ra2, Y - 1).astype(jnp.bfloat16)
    a3 = []
    for r in rest("x"):
        to, at = place.along("x", r)
        a3.append(copies.start(sa2.at[at], ra3.at[r - 1], to))

    iswap.wait_recv()
    for b in range(16):
        block = slice(b * 128, (b + 1) * 128)
        mine = pl.ds(pl.multiple_of(b * 256 + core * 128, 128), 128)
        theirs = pl.ds(pl.multiple_of(b * 256 + other * 128, 128), 128)
        ig_ref[:, mine] = igs[here, block]
        ig_ref[:, theirs] = igr[:, block]
    for copy in b3:
        copy.wait_recv()
    wgrad_ref[:, 0:256] = add_up(sb2[z], rb3, Z - 1)
    for copy in g3:
        copy.wait_recv()
    wgrad_ref[:, 256:512] = add_up(sg2[z], rg3, Z - 1)
    for copy in a3:
        copy.wait_recv()
    last = add_up(sa2[x], ra3, X - 1)
    wgrad_ref[:, 512:1024] = jnp.dot(
        last, readout[...], precision=HIGH, preferred_element_type=f32
    )
    for stream in streams:
        stream.close()
    copies.close()


def reduce(far, near, w, wb, wg, wa, wd, tb, vfull):
    f32, low = jnp.float32, jnp.bfloat16
    return pl.pallas_call(
        reduce_kernel,
        out_shape=(shape((ROWS, 4096)), shape((16, 1024), f32)),
        in_specs=[ANY] * 9,
        out_specs=(VMEM, VMEM),
        scratch_shapes=[
            pltpu.VMEM((Z, YH, X, YL, 16, 256), low),
            pltpu.VMEM((Z, YH, X, YL, 16, 256), low),
            pltpu.VMEM((Z, YH, X, YL, 16, 384), low),
            pltpu.VMEM((Z, YH, X, YL, 16, 128), low),
            pltpu.VMEM((2 * ROWS, 2048), low),
            pltpu.VMEM((SP, 8, D), f32),
            pltpu.VMEM((WIN - ROWS, KV * D), low),
            pltpu.VMEM((HEADS, WIN), f32),
            pltpu.VMEM((128, KV * D), f32),
            pltpu.VMEM((2, ROWS, KV * D), low),
            pltpu.VMEM((2, ROWS, KV * D), low),
            pltpu.VMEM((ROWS, KV * D), low),
            pltpu.VMEM((ROWS, KV * D), low),
            pltpu.VMEM((2, HEADS, ROWS), f32),
            pltpu.VMEM((2, HEADS, ROWS), f32),
            pltpu.VMEM((HEADS, ROWS), f32),
            pltpu.VMEM((HEADS, ROWS), f32),
            pltpu.VMEM((ROWS, KV * D), f32),
            pltpu.VMEM((HEADS, ROWS), f32),
            pltpu.VMEM((2 * ROWS, 1152), low),
            pltpu.VMEM((Z, YH, X, YL, 16, 256), low),
            pltpu.VMEM((Z, YH, X, YL, 16, 256), low),
            pltpu.VMEM((Z, YH, X, YL, 16, 128), low),
            pltpu.VMEM((X - 1, Z, YH, YL, 16, 256), low),
            pltpu.VMEM((Y - 1, Z, 16, 256), low),
            pltpu.VMEM((Z - 1, 16, 256), low),
            pltpu.VMEM((Y - 1, Z, X, 16, 256), low),
            pltpu.VMEM((X - 1, Z, 16, 256), low),
            pltpu.VMEM((Z - 1, 16, 256), low),
            pltpu.VMEM((Z - 1, YH, X, YL, 16, 128), low),
            pltpu.VMEM((Y - 1, X, 16, 128), low),
            pltpu.VMEM((X - 1, 16, 128), low),
            pltpu.VMEM((Z, YH, YL, 16, 256), low),
            pltpu.VMEM((Z, 16, 256), low),
            pltpu.VMEM((Z, X, 16, 256), low),
            pltpu.VMEM((Z, 16, 256), low),
            pltpu.VMEM((YH, X, YL, 16, 128), low),
            pltpu.VMEM((X, 16, 128), low),
            pltpu.VMEM((2 * ROWS, 2048), low),
            pltpu.VMEM((ROWS, 2048), low),
            pltpu.SemaphoreType.DMA((64,)),
            pltpu.SemaphoreType.DMA((64,)),
            pltpu.SemaphoreType.DMA((10,)),
        ],
        compiler_params=pltpu.CompilerParams(
            collective_id=1, has_side_effects=True, vmem_limit_bytes=60 * 2**20
        ),
    )(far, near, w, wb, wg, wa, wd, tb, vfull)


def on_device(tokens, queries, kv_weight, vhm, lengths, positions, returns):
    vhm = vhm.reshape(HEADS // SP, D)
    kwin, vwin, vfull, wb, wg, wa, wd, tb = gather(tokens, kv_weight, vhm)
    dq, far, near, w = attention(lengths, positions, returns, queries, kwin, vwin, vfull)
    input_grad, weight_grad = reduce(far, near, w, wb, wg, wa, wd, tb, vfull)
    return dq, input_grad, weight_grad


def solution(mesh):
    rows = P(("fsdp", "sp"), None)
    slab = P("fsdp", None)
    return jax.shard_map(
        on_device,
        mesh=mesh,
        in_specs=(rows, rows, rows, P("sp"), slab, slab, slab),
        out_specs=(rows, rows, rows),
        check_vma=False,
    )
```

```python
import math

import jax
import jax.numpy as jnp
from jax import lax
from jax.experimental import pallas as pl
from jax.experimental.pallas import tpu as pltpu
from jax.sharding import PartitionSpec as P

HEADS = 40
KV = 4
GROUP = 10
D = 128
SCALE = 1.0 / math.sqrt(D)
ROWS = 128
WIN = 640
TILE = 48
PADDED = 144
NEG = -1e30
HIGH = lax.Precision.HIGHEST


def tdot(a, b, precision=None):
    return lax.dot_general(
        a, b, (((0,), (0,)), ((), ())), precision=precision, preferred_element_type=jnp.float32
    )


def ndot(a, b):
    return lax.dot_general(a, b, (((1,), (1,)), ((), ())), preferred_element_type=jnp.float32)


def attention_kernel(
    len_hbm, pos_hbm, ret_hbm, q_hbm, k_hbm, v_hbm, vhm_hbm, dq_hbm, far_hbm, near_hbm, w_hbm,
    len_ref, pos_ref, ret_ref, q_ref, k_ref, v_ref, vhm_ref,
    qc, dqc, props, probs, heads, dk_ref, u_ref, far_ref, w_ref, dq_ref, sems, qsems,
):
    base = lax.axis_index("sp") * ROWS
    moves = [
        pltpu.make_async_copy(src, dst, sems.at[i])
        for i, (src, dst) in enumerate(
            (
                (len_hbm, len_ref), (pos_hbm, pos_ref), (ret_hbm, ret_ref),
                (vhm_hbm, vhm_ref), (v_hbm, v_ref), (k_hbm, k_ref),
            )
        )
    ]
    chunks = [slice(c * GROUP * D, (c + 1) * GROUP * D) for c in range(KV)]
    quest = [
        pltpu.make_async_copy(q_hbm.at[:, cols], q_ref.at[:, cols], qsems.at[c])
        for c, cols in enumerate(chunks)
    ]
    for move in moves[:3] + quest + moves[3:]:
        move.start()
    dqc[...] = jnp.zeros_like(dqc)
    dk_ref[...] = jnp.zeros_like(dk_ref)
    w_ref[...] = jnp.zeros_like(w_ref)
    for move in moves[:3]:
        move.wait()
    rows = base + lax.broadcasted_iota(jnp.int32, (ROWS, 1), 0)
    hits = (rows == pos_ref[...]).astype(jnp.float32)
    count = jnp.sum(hits, axis=1, keepdims=True)
    total_ret = jnp.sum(hits * ret_ref[...], axis=1, keepdims=True)
    marked = (count > 0).astype(jnp.float32)
    tri = (
        lax.broadcasted_iota(jnp.int32, (ROWS, ROWS), 1)
        <= lax.broadcasted_iota(jnp.int32, (ROWS, ROWS), 0)
    ).astype(jnp.bfloat16)
    rank = jnp.dot(
        tri, jnp.broadcast_to(marked, (ROWS, D)).astype(jnp.bfloat16),
        preferred_element_type=jnp.float32,
    )
    n = jnp.sum(marked).astype(jnp.int32)
    slots = lax.broadcasted_iota(jnp.int32, (ROWS, ROWS), 1)
    pick = ((rank.astype(jnp.int32) - 1 == slots) & (marked > 0)).astype(jnp.float32)
    lane = lax.broadcasted_iota(jnp.int32, (ROWS, D), 1)
    b1 = len_ref[:, 0:1]
    b2 = b1 + len_ref[:, 1:2]
    b3 = b2 + len_ref[:, 2:3]
    start = jnp.where(rows >= b3, b3, jnp.where(rows >= b2, b2, jnp.where(rows >= b1, b1, 0)))
    fields = jnp.where(lane == 0, count, 0.0)
    fields = jnp.where(lane == 1, total_ret, fields)
    fields = jnp.where(lane == 2, rows.astype(jnp.float32), fields)
    fields = jnp.where(lane == 3, start.astype(jnp.float32), fields)
    props[0:ROWS, :] = tdot(pick, fields, HIGH)
    props[ROWS:, :] = jnp.zeros((PADDED - ROWS, D), jnp.float32)
    pick_low = pick.astype(jnp.bfloat16)
    qc[ROWS:, :] = jnp.zeros((PADDED - ROWS, HEADS * D), jnp.bfloat16)
    for c, cols in enumerate(chunks):
        quest[c].wait()
        qc[0:ROWS, cols] = tdot(pick_low, q_ref[:, cols]).astype(jnp.bfloat16)
    for move in moves[3:]:
        move.wait()
    for c in range(KV):
        readout = jnp.concatenate(
            [vhm_ref[h // 5, h % 5 : h % 5 + 1, :] for h in range(c * GROUP, (c + 1) * GROUP)]
            + [jnp.zeros((6, D), jnp.float32)], axis=0,
        )
        high = readout.astype(jnp.bfloat16)
        rest = readout - high.astype(jnp.float32)
        mid = rest.astype(jnp.bfloat16)
        low = (rest - mid.astype(jnp.float32)).astype(jnp.bfloat16)
        values = v_ref[:, c * D : (c + 1) * D]
        u_ref[c] = ndot(high, values) + (ndot(mid, values) + ndot(low, values))
    places = (base - 512) + lax.broadcasted_iota(jnp.int32, (1, WIN), 1)

    @pl.loop(0, (n + TILE - 1) // TILE)
    def _(t):
        at = pl.ds(pl.multiple_of(t * TILE, 16), TILE)
        prop = props[at, :]
        cnt, ret = prop[:, 0:1], prop[:, 1:2]
        row, low = prop[:, 2:3].astype(jnp.int32), prop[:, 3:4].astype(jnp.int32)
        allowed = (places >= low) & (places <= row)
        estimate = jnp.zeros((TILE, 1), jnp.float32)
        for c in range(KV):
            keys = k_ref[:, c * D : (c + 1) * D]
            q = jnp.concatenate(
                [qc[at, (c * GROUP + g) * D : (c * GROUP + g + 1) * D] for g in range(GROUP)], axis=0
            )
            scores = ndot(q, keys) * SCALE
            for g in range(GROUP):
                h = c * GROUP + g
                s = jnp.where(allowed, scores[g * TILE : (g + 1) * TILE, :], NEG)
                e = jnp.exp(s - jnp.max(s, axis=1, keepdims=True))
                p = e * (1.0 / jnp.sum(e, axis=1, keepdims=True))
                probs[h] = p
                low_p = p.astype(jnp.bfloat16).astype(jnp.float32)
                hv = jnp.sum(low_p * u_ref[c, g : g + 1, :], axis=1, keepdims=True)
                heads[h] = hv
                estimate = estimate + hv
        coef = cnt * estimate - ret
        for c in range(KV):
            keys = k_ref[:, c * D : (c + 1) * D]
            q = jnp.concatenate(
                [qc[at, (c * GROUP + g) * D : (c * GROUP + g + 1) * D] for g in range(GROUP)], axis=0
            )
            values = v_ref[:, c * D : (c + 1) * D]
            grad_out = jnp.concatenate(
                [
                    (coef * vhm_ref[h // 5, h % 5 : h % 5 + 1, :]).astype(jnp.bfloat16)
                    for h in range(c * GROUP, (c + 1) * GROUP)
                ],
                axis=0,
            )
            grad_probs = ndot(grad_out, values)
            parts = []
            for g in range(GROUP):
                h = c * GROUP + g
                p = probs[h]
                low_p = p.astype(jnp.bfloat16).astype(jnp.float32)
                w_ref[h : h + 1, :] += jnp.sum(low_p * coef, axis=0, keepdims=True)
                grad_p = grad_probs[g * TILE : (g + 1) * TILE, :]
                parts.append((p * (grad_p - coef * heads[h])).astype(jnp.bfloat16))
            gs = jnp.concatenate(parts, axis=0)
            dq = (jnp.dot(gs, keys, preferred_element_type=jnp.float32) * SCALE).astype(jnp.bfloat16)
            for g in range(GROUP):
                h = c * GROUP + g
                dqc[at, h * D : (h + 1) * D] = dq[g * TILE : (g + 1) * TILE, :]
            dk_ref[:, c * D : (c + 1) * D] += tdot(gs, q) * SCALE

    far_ref[...] = dk_ref[: WIN - ROWS, :].astype(jnp.bfloat16)
    moves = [
        pltpu.make_async_copy(far_ref, far_hbm, sems.at[0]),
        pltpu.make_async_copy(dk_ref.at[WIN - ROWS :, :], near_hbm, sems.at[1]),
        pltpu.make_async_copy(w_ref, w_hbm, sems.at[2]),
    ]
    for move in moves:
        move.start()
    for c, cols in enumerate(chunks):
        dq_ref[:, cols] = jnp.dot(
            pick_low, dqc[0:ROWS, cols], preferred_element_type=jnp.float32
        ).astype(jnp.bfloat16)
        out = pltpu.make_async_copy(dq_ref.at[:, cols], dq_hbm.at[:, cols], qsems.at[c])
        out.start()
        moves.append(out)
    for move in moves:
        move.wait()


VMEM = pl.BlockSpec(memory_space=pltpu.VMEM)
ANY = pl.BlockSpec(memory_space=pl.ANY)


def shape(dims, kind=jnp.bfloat16):
    return jax.ShapeDtypeStruct(dims, kind)


def attention(lengths, positions, returns, queries, keys, values, vhm):
    return pl.pallas_call(
        attention_kernel,
        out_shape=(
            shape((ROWS, HEADS * D)),
            shape((WIN - ROWS, KV * D)),
            shape((ROWS, KV * D), jnp.float32),
            shape((HEADS, WIN), jnp.float32),
        ),
        in_specs=[ANY] * 7,
        out_specs=(ANY,) * 4,
        scratch_shapes=[
            pltpu.VMEM((1, 4), jnp.int32),
            pltpu.VMEM((1, 256), jnp.int32),
            pltpu.VMEM((1, 256), jnp.float32),
            pltpu.VMEM((ROWS, HEADS * D), jnp.bfloat16),
            pltpu.VMEM((WIN, KV * D), jnp.bfloat16),
            pltpu.VMEM((WIN, KV * D), jnp.bfloat16),
            pltpu.VMEM((SP, 8, D), jnp.float32),
            pltpu.VMEM((PADDED, HEADS * D), jnp.bfloat16),
            pltpu.VMEM((PADDED, HEADS * D), jnp.bfloat16),
            pltpu.VMEM((PADDED, D), jnp.float32),
            pltpu.VMEM((HEADS, TILE, WIN), jnp.float32),
            pltpu.VMEM((HEADS, TILE, 1), jnp.float32),
            pltpu.VMEM((WIN, KV * D), jnp.float32),
            pltpu.VMEM((KV, 16, WIN), jnp.float32),
            pltpu.VMEM((WIN - ROWS, KV * D), jnp.bfloat16),
            pltpu.VMEM((HEADS, WIN), jnp.float32),
            pltpu.VMEM((ROWS, HEADS * D), jnp.bfloat16),
            pltpu.SemaphoreType.DMA((6,)),
            pltpu.SemaphoreType.DMA((4,)),
        ],
        compiler_params=pltpu.CompilerParams(vmem_limit_bytes=60 * 2**20),
    )(lengths, positions, returns, queries, keys, values, vhm)


MESH = pl.DeviceIdType.MESH
Z, YH, X, YL = 8, 2, 4, 2
Y = YH * YL
SP = X * YL
BACK = 4


class Place:
    def __init__(self):
        fsdp, self.sp = lax.axis_index("fsdp"), lax.axis_index("sp")
        self.core = fsdp % 2
        self.yh = (fsdp // 2) % YH
        self.z = fsdp // 4
        self.x, self.yl = self.sp // YL, self.sp % YL
        self.y = self.yh * YL + self.yl

    def at(self, z=None, yh=None, core=None, x=None, yl=None):
        z = self.z if z is None else z
        yh = self.yh if yh is None else yh
        core = self.core if core is None else core
        x = self.x if x is None else x
        yl = self.yl if yl is None else yl
        return (z * 4 + yh * 2 + core, x * YL + yl)

    def partner(self):
        return self.at(core=1 - self.core)

    def along(self, axis, r):
        if axis == "x":
            x = (self.x + r) % X
            return self.at(x=x), x
        if axis == "z":
            z = (self.z + r) % Z
            return self.at(z=z), z
        y = (self.y + r) % Y
        return self.at(yh=y // YL, yl=y % YL), y

    def slab(self, r):
        return (lax.axis_index("fsdp"), (self.sp + r) % SP)


COUNT = {"x": X, "y": Y, "z": Z}


class Copies:
    def __init__(self, send, recv):
        self.send, self.recv, self.used, self.open = send, recv, 0, []

    def make(self, src, dst, to):
        i = self.used
        self.used += 1
        return pltpu.make_async_remote_copy(
            src_ref=src, dst_ref=dst, send_sem=self.send.at[i], recv_sem=self.recv.at[i],
            device_id=to, device_id_type=MESH,
        )

    def start(self, src, dst, to):
        copy = self.make(src, dst, to)
        copy.start()
        self.open.append(copy)
        return copy

    def close(self):
        for copy in self.open:
            copy.wait_send()


class Ring4:
    def __init__(self, copies, place, axis, view):
        self.copies, self.view = copies, view
        self.right, _ = place.along(axis, 1)
        self.left, _ = place.along(axis, 3)
        at = getattr(place, axis)
        self.at = [at, (at + 3) % 4, (at + 1) % 4]

    def send(self, at, half, to):
        view = self.view(at, half)
        return self.copies.start(view, view, to)

    def start(self):
        one, two = slice(0, Z // 2), slice(Z // 2, Z)
        self.a = [self.send(self.at[0], h, self.right) for h in (one, two)]
        self.b = [self.send(self.at[0], h, self.left) for h in (two, one)]

    def mid(self):
        self.a[0].wait_recv()
        self.c = self.send(self.at[1], slice(0, Z // 2), self.right)
        self.b[0].wait_recv()
        self.d = self.send(self.at[2], slice(Z // 2, Z), self.left)

    def end(self):
        for copy in (self.a[1], self.b[1], self.c, self.d):
            copy.wait_recv()


class Ring8:
    def __init__(self, copies, place, ref):
        self.copies, self.ref, self.z = copies, ref, place.z
        self.right, _ = place.along("z", 1)
        self.left, _ = place.along("z", Z - 1)
        self.k = 0

    def send(self, at, half, to):
        view = self.ref.at[at, half]
        return self.copies.start(view, view, to)

    def start(self):
        self.a = [self.send(self.z, h, self.right) for h in (0, 1)]
        self.b = [self.send(self.z, h, self.left) for h in (1, 0)]

    def step(self):
        self.k += 1
        last = self.k == Z // 2 - 1
        a, b = self.a, self.b
        self.a, self.b = [], []
        for i, (right, left) in enumerate(((0, 1), (1, 0))):
            a[i].wait_recv()
            if i == 0 or not last:
                self.a.append(self.send((self.z + Z - self.k) % Z, right, self.right))
            b[i].wait_recv()
            if i == 0 or not last:
                self.b.append(self.send((self.z + self.k) % Z, left, self.left))

    def end(self):
        for copy in self.a + self.b:
            copy.wait_recv()


def slot(d):
    return slice((BACK - d) * ROWS, (BACK - d + 1) * ROWS)


class Window:
    def __init__(self, copies, place, ref, columns):
        x, yl = place.x, place.yl
        one, two = place.at(x=(x + 1) % X), place.at(x=(x + 2) % X)
        top, bottom = place.at(yl=1), place.at(yl=0)
        row = [slot(d) for d in range(BACK + 1)]

        def move(src, dst, to, sends, takes):
            return copies.make(ref.at[row[src], columns], ref.at[row[dst], columns], to), sends, takes

        self.m1 = move(0, 1, top, yl == 0, yl == 1)
        self.m2 = move(0, 2, one, x + 1 < X, x >= 1)
        self.m4 = move(0, 4, two, x + 2 < X, x >= 2)
        self.f1 = move(2, 1, bottom, (yl == 1) & (x >= 1), (yl == 0) & (x >= 1))
        self.f3 = move(2, 3, top, (yl == 0) & (x >= 1), (yl == 1) & (x >= 1))
        self.g3 = move(4, 3, bottom, (yl == 1) & (x >= 2), (yl == 0) & (x >= 2))

    def start(self):
        for copy, sends, _ in (self.m2, self.m4, self.m1):
            pl.when(sends)(copy.start)

    def mid(self):
        copy, _, takes = self.m2
        pl.when(takes)(copy.wait_recv)
        for copy, sends, _ in (self.f1, self.f3):
            pl.when(sends)(copy.start)
        copy, _, takes = self.m4
        pl.when(takes)(copy.wait_recv)
        copy, sends, _ = self.g3
        pl.when(sends)(copy.start)

    def end(self):
        for copy, _, takes in (self.m1, self.f1, self.f3, self.g3):
            pl.when(takes)(copy.wait_recv)
        for copy, sends, _ in (self.m1, self.m2, self.m4, self.f1, self.f3, self.g3):
            pl.when(sends)(copy.wait_send)


def greet(place):
    barrier = pltpu.get_barrier_semaphore()
    peers = [place.partner()]
    for axis in ("x", "y", "z"):
        peers += [place.along(axis, r)[0] for r in range(1, COUNT[axis])]
    peers += [place.at(x=(place.x + r) % X, yl=1 - place.yl) for r in range(1, X)]
    for peer in peers:
        pl.semaphore_signal(barrier, inc=1, device_id=peer, device_id_type=MESH)
    pl.semaphore_wait(barrier, len(peers))


class Return:
    def __init__(self, copies, place, out, have, by_y, by_x, sum2, sum4, total, columns):
        x, yl = place.x, place.yl
        self.x, self.yl, self.have = x, yl, have
        self.total = total.at[:, columns]
        self.ya, self.yb = by_y.at[0, :, columns], by_y.at[1, :, columns]
        self.xa, self.xb = by_x.at[0, :, columns], by_x.at[1, :, columns]
        self.sum2, self.sum4 = sum2.at[:, columns], sum4.at[:, columns]
        across = place.at(yl=1 - yl)
        one, two = place.at(x=(x + X - 1) % X), place.at(x=(x + X - 2) % X)
        self.top, self.bottom = yl == 1, yl == 0
        self.a = copies.make(out(1), self.ya, across)
        self.b = copies.make(out(3), self.yb, across)
        self.c = copies.make(self.sum2, self.xa, one)
        self.d = copies.make(self.sum4, self.xb, two)
        self.a_sends = self.top | (x >= 1)
        self.b_sends = (self.top & (x >= 1)) | (self.bottom & (x >= 2))
        self.b_takes = (self.bottom & (x >= 1)) | (self.top & (x >= 2))
        self.a_takes = self.bottom | (x >= 1)

    def start(self):
        pl.when(self.a_sends)(self.a.start)
        pl.when(self.b_sends)(self.b.start)

    def add(self, condition, to, what):
        @pl.when(condition)
        def _():
            to[...] = (to[...].astype(jnp.float32) + what[...].astype(jnp.float32)).astype(to.dtype)

    def mid(self):
        x = self.x
        self.sum2[...] = self.have(2)[...]
        self.sum4[...] = self.have(4)[...]
        pl.when(self.a_takes)(self.a.wait_recv)
        pl.when(self.b_takes)(self.b.wait_recv)
        self.add(self.bottom & (x >= 1), self.sum2, self.yb)
        self.add(self.top & (x >= 1), self.sum2, self.ya)
        self.add(self.top & (x >= 2), self.sum4, self.yb)
        self.add(self.bottom, self.total, self.ya)
        pl.when(x >= 1)(self.c.start)
        pl.when(x >= 2)(self.d.start)

    def end(self):
        x = self.x
        pl.when(x + 1 < X)(self.c.wait_recv)
        self.add(x + 1 < X, self.total, self.xa)
        pl.when(x + 2 < X)(self.d.wait_recv)
        self.add(x + 2 < X, self.total, self.xb)

    def close(self):
        x = self.x
        pl.when(self.a_sends)(self.a.wait_send)
        pl.when(self.b_sends)(self.b.wait_send)
        pl.when(x >= 1)(self.c.wait_send)
        pl.when(x >= 2)(self.d.wait_send)


def gather_kernel(
    t_hbm, kv_ref, vhm_ref,
    kwin, vwin, vfull, wb_hbm, wg_hbm, wa_hbm, wd_hbm, tb_hbm,
    t_ref, wb, wg, wa, wd, tb, tsend, pk, pv, pink, pinv, ssem, rsem, lsem,
):
    place = Place()
    copies = Copies(ssem, rsem)
    z, yh, x, yl, core, j = place.z, place.yh, place.x, place.yl, place.core, place.sp
    other = 1 - core
    fetch = pltpu.make_async_copy(t_hbm, t_ref, lsem.at[0])
    fetch.start()

    wb[z, yh, x, yl] = kv_ref[:, 0:256]
    wg[z, yh, x, yl] = kv_ref[:, 256:512]
    wa[z, yh, x, yl] = kv_ref[:, 512:896]
    wd[z, yh, x, yl] = kv_ref[:, 896:1024]
    vfull[j] = jnp.zeros((8, D), jnp.float32)
    vfull[j, 0 : HEADS // SP, :] = vhm_ref[...]
    here = pl.ds(pl.multiple_of(core * ROWS, ROWS), ROWS)
    there = pl.ds(pl.multiple_of(other * ROWS, ROWS), ROWS)

    greet(place)

    def spread(axis, view):
        return [
            copies.start(view, view, place.along(axis, r)[0]) for r in range(1, COUNT[axis])
        ]

    def arrive(group):
        for copy in group:
            copy.wait_recv()

    a1 = spread("x", wa.at[z, yh, x, yl])
    b1 = spread("z", wb.at[z, yh, x, yl])
    g1 = spread("z", wg.at[z, yh, x, yl])
    d1 = spread("z", wd.at[z, yh, x, yl])
    v1 = [copies.start(vfull.at[j], vfull.at[j], place.slab(r)) for r in range(1, SP)]
    b3 = Ring4(copies, place, "x", lambda x, h: wb.at[h, :, x])
    g3 = Ring4(copies, place, "y", lambda y, h: wg.at[h, y // YL, :, y % YL])
    d3 = Ring4(copies, place, "y", lambda y, h: wd.at[h, y // YL, :, y % YL])
    a3 = Ring8(copies, place, wa)

    fetch.wait()
    for b in range(16):
        mine = pl.ds(pl.multiple_of(b * 256 + core * 128, 128), 128)
        theirs = pl.ds(pl.multiple_of(b * 256 + other * 128, 128), 128)
        tb[here, b * 128 : (b + 1) * 128] = t_ref[:, mine]
        tsend[:, b * 128 : (b + 1) * 128] = t_ref[:, theirs]
    tswap = copies.start(tsend, tb.at[here, :], place.partner())

    arrive(a1)
    a2 = spread("y", wa.at[z, yh, :, yl])
    arrive(b1)
    b2 = spread("y", wb.at[:, yh, x, yl])
    arrive(g1)
    g2 = spread("x", wg.at[:, yh, x, yl])
    arrive(a2)
    a3.start()
    arrive(d1)
    d2 = spread("x", wd.at[:, yh, x, yl])
    arrive(b2)
    b3.start()
    arrive(g2)
    g3.start()
    arrive(d2)
    for d in range(1, BACK + 1):

        @pl.when(j - d < 0)
        def _():
            kwin[slot(d), :] = jnp.zeros((ROWS, KV * D), jnp.bfloat16)
            vwin[slot(d), :] = jnp.zeros((ROWS, KV * D), jnp.bfloat16)

    a3.step()
    arrive([tswap])
    b3.mid()
    g3.mid()
    d3.start()
    a3.step()
    b3.end()
    pk[:, 0:256] = jnp.dot(
        tb[...], wb[...].reshape(2048, 256), preferred_element_type=jnp.float32
    )
    g3.end()
    pk[:, 256:512] = jnp.dot(
        tb[...], wg[...].reshape(2048, 256), preferred_element_type=jnp.float32
    )
    kswap = copies.start(pk.at[there, :], pink, place.partner())
    d3.mid()
    a3.step()
    keep = [
        pltpu.make_async_copy(src, dst, lsem.at[i])
        for i, (src, dst) in enumerate(((tb, tb_hbm), (wb, wb_hbm), (wg, wg_hbm), (wa, wa_hbm), (wd, wd_hbm)))
    ]
    for copy in keep[:3]:
        copy.start()
    arrive([kswap])
    kwin[slot(0), :] = (pk[here, :] + pink[...]).astype(jnp.bfloat16)
    keys = Window(copies, place, kwin, slice(None))
    parts = [slice(384, 512), slice(0, 256), slice(256, 384)]
    values = [Window(copies, place, vwin, columns) for columns in parts]
    keys.start()

    def swap_values(columns):
        return copies.start(pv.at[there, columns], pinv.at[:, columns], place.partner())

    def set_values(columns):
        vwin[slot(0), columns] = (pv[here, columns] + pinv[:, columns]).astype(jnp.bfloat16)

    d3.end()
    keep[4].start()
    pv[:, 384:512] = jnp.dot(
        tb[...], wd[...].reshape(2048, 128), preferred_element_type=jnp.float32
    )
    vswap = swap_values(parts[0])
    arrive([vswap])
    set_values(parts[0])
    values[0].start()
    a3.end()
    keep[3].start()
    pv[:, 0:384] = jnp.dot(
        tb[...], wa[...].reshape(2048, 384), preferred_element_type=jnp.float32
    )
    vswap = swap_values(slice(0, 384))
    keys.mid()
    arrive([vswap])
    for columns, window in zip(parts[1:], values[1:]):
        set_values(columns)
        window.start()
    for window in values:
        window.mid()
    arrive(v1)
    keys.end()
    for window in values:
        window.end()
    copies.close()
    for copy in keep:
        copy.wait()


def gather(tokens, kv_weight, vhm):
    f32, low = jnp.float32, jnp.bfloat16
    return pl.pallas_call(
        gather_kernel,
        out_shape=(
            shape((WIN, KV * D)),
            shape((WIN, KV * D)),
            shape((SP, 8, D), f32),
            shape((Z, YH, X, YL, 16, 256)),
            shape((Z, YH, X, YL, 16, 256)),
            shape((Z, YH, X, YL, 16, 384)),
            shape((Z, YH, X, YL, 16, 128)),
            shape((2 * ROWS, 2048)),
        ),
        in_specs=[ANY, VMEM, VMEM],
        out_specs=(VMEM, VMEM, VMEM) + (ANY,) * 5,
        scratch_shapes=[
            pltpu.VMEM((ROWS, 4096), low),
            pltpu.VMEM((Z, YH, X, YL, 16, 256), low),
            pltpu.VMEM((Z, YH, X, YL, 16, 256), low),
            pltpu.VMEM((Z, YH, X, YL, 16, 384), low),
            pltpu.VMEM((Z, YH, X, YL, 16, 128), low),
            pltpu.VMEM((2 * ROWS, 2048), low),
            pltpu.VMEM((ROWS, 2048), low),
            pltpu.VMEM((2 * ROWS, 512), f32),
            pltpu.VMEM((2 * ROWS, 512), f32),
            pltpu.VMEM((ROWS, 512), f32),
            pltpu.VMEM((ROWS, 512), f32),
            pltpu.SemaphoreType.DMA((112,)),
            pltpu.SemaphoreType.DMA((112,)),
            pltpu.SemaphoreType.DMA((5,)),
        ],
        compiler_params=pltpu.CompilerParams(
            collective_id=0, has_side_effects=True, vmem_limit_bytes=60 * 2**20
        ),
    )(tokens, kv_weight, vhm)


def reduce_kernel(
    far_ref, near_hbm, w_ref, wb_hbm, wg_hbm, wa_hbm, wd_hbm, tb_hbm, vfull_hbm,
    ig_hbm, wgrad_ref,
    ig_ref, wb, wg, wa, wd, tb, vfull, far, wfar, readout, ky, kx, k2, k4, wy, wx, w2, w4, gk, gw, gb, pb, pg, pa,
    rb1, rb2, rb3, rg1, rg2, rg3, ra1, ra2, ra3,
    sb1, sb2, sg1, sg2, sa1, sa2, igs, igr, ssem, rsem, lsem,
):
    place = Place()
    copies = Copies(ssem, rsem)
    z, yh, x, yl, core, j = place.z, place.yh, place.x, place.yl, place.core, place.sp
    other = 1 - core
    f32 = jnp.float32
    here = pl.ds(pl.multiple_of(core * ROWS, ROWS), ROWS)
    there = pl.ds(pl.multiple_of(other * ROWS, ROWS), ROWS)
    copied = (
        (near_hbm, gk), (w_ref.at[:, WIN - ROWS :], gw), (vfull_hbm, vfull),
        (far_ref, far), (w_ref, wfar),
        (tb_hbm, tb), (wb_hbm, wb), (wg_hbm, wg), (wa_hbm, wa), (wd_hbm, wd),
    )
    fetch = [
        pltpu.make_async_copy(src, dst, lsem.at[i])
        for i, (src, dst) in enumerate(copied)
    ]
    for copy in fetch:
        copy.start()
    greet(place)

    first, second = slice(0, 256), slice(256, 512)
    everything = slice(None)
    streams = [
        Return(
            copies, place,
            lambda d: w_ref.at[:, slot(d)], lambda d: wfar.at[:, slot(d)], wy, wx, w2, w4, gw,
            everything,
        )
    ]
    for columns in (first, second):
        streams.append(
            Return(
                copies, place,
                lambda d, columns=columns: far_ref.at[slot(d), columns],
                lambda d, columns=columns: far.at[slot(d), columns],
                ky, kx, k2, k4, gk, columns,
            )
        )
    for stream in streams:
        stream.start()

    def rest(axis):
        return range(1, COUNT[axis])

    def add_up(own, slots, n):
        total = own.astype(f32)
        for k in range(n):
            total = total + slots[k].astype(f32)
        return total

    def swap(columns):
        view = gb.at[here, columns]
        return copies.start(view, view, place.partner())

    def keys_arrive(stream, columns):
        stream.end()
        gb[here, columns] = gk[:, columns].astype(jnp.bfloat16)
        return swap(columns)

    readout[...] = jnp.zeros_like(readout)
    for copy in fetch[2:3]:
        copy.wait()
    for h in range(HEADS):
        c = h // GROUP
        readout[h : h + 1, c * D : (c + 1) * D] = vfull[h // 5, h % 5 : h % 5 + 1, :]
    for copy in fetch[0:2] + fetch[3:5]:
        copy.wait()
    for stream in streams:
        stream.mid()
    streams[0].end()
    whi = gw[...].astype(jnp.bfloat16).astype(f32)
    wlo = gw[...] - whi
    stacked = jnp.concatenate([whi, wlo, jnp.zeros((48, ROWS), f32)], axis=0)
    gb[here, 1024:1152] = stacked.T.astype(jnp.bfloat16)
    gb[here, 512:1024] = lax.dot_general(
        gw[...], readout[0:HEADS, :], (((0,), (0,)), ((), ())), precision=HIGH,
        preferred_element_type=f32,
    ).astype(jnp.bfloat16)
    swap_w = swap(slice(512, 1152))
    for copy in fetch[5:]:
        copy.wait()
    swap_w.wait_recv()
    for n in range(Z):
        part = tdot(tb[:, n * 256 : (n + 1) * 256], gb[:, 1024:1152])
        part = part + pltpu.roll(part, 128 - 40, 1)
        pa[n] = part.astype(jnp.bfloat16).reshape(YH, X, YL, 16, 128)
    a1 = []
    for r in rest("z"):
        to, at = place.along("z", r)
        a1.append(copies.start(pa.at[at], ra1.at[r - 1], to))
    swap_b = keys_arrive(streams[1], first)
    swap_b.wait_recv()
    for n in range(Z):
        part = tdot(tb[:, n * 256 : (n + 1) * 256], gb[:, 0:256])
        pb[n] = part.astype(jnp.bfloat16).reshape(YH, X, YL, 16, 256)
    b1 = []
    for r in rest("x"):
        to, at = place.along("x", r)
        b1.append(copies.start(pb.at[:, :, at], rb1.at[r - 1], to))
    swap_g = keys_arrive(streams[2], second)
    swap_g.wait_recv()
    for n in range(Z):
        part = tdot(tb[:, n * 256 : (n + 1) * 256], gb[:, 256:512])
        pg[n] = part.astype(jnp.bfloat16).reshape(YH, X, YL, 16, 256)
    g1 = []
    for r in rest("y"):
        to, at = place.along("y", r)
        g1.append(copies.start(pg.at[:, at // YL, :, at % YL], rg1.at[r - 1], to))

    for n in range(Z):
        part = ndot(gb[:, 0:256], wb[n].reshape(256, 256))
        part = part + ndot(gb[:, 256:512], wg[n].reshape(256, 256))
        part = part + ndot(gb[:, 512:896], wa[n].reshape(256, 384))
        part = part + ndot(gb[:, 896:1024], wd[n].reshape(256, 128))
        igs[:, n * 256 : (n + 1) * 256] = part.astype(jnp.bfloat16)
    iswap = copies.start(igs.at[there, :], igr, place.partner())

    for copy in b1:
        copy.wait_recv()
    sb1[...] = add_up(pb[:, :, x], rb1, X - 1).astype(jnp.bfloat16)
    b2 = []
    for r in rest("y"):
        to, at = place.along("y", r)
        b2.append(copies.start(sb1.at[:, at // YL, at % YL], rb2.at[r - 1], to))
    for copy in g1:
        copy.wait_recv()
    sg1[...] = add_up(pg[:, yh, :, yl], rg1, Y - 1).astype(jnp.bfloat16)
    g2 = []
    for r in rest("x"):
        to, at = place.along("x", r)
        g2.append(copies.start(sg1.at[:, at], rg2.at[r - 1], to))
    for copy in a1:
        copy.wait_recv()
    sa1[...] = add_up(pa[z], ra1, Z - 1).astype(jnp.bfloat16)
    a2 = []
    for r in rest("y"):
        to, at = place.along("y", r)
        a2.append(copies.start(sa1.at[at // YL, :, at % YL], ra2.at[r - 1], to))
    for copy in b2:
        copy.wait_recv()
    sb2[...] = add_up(sb1[:, yh, yl], rb2, Y - 1).astype(jnp.bfloat16)
    b3 = []
    for r in rest("z"):
        to, at = place.along("z", r)
        b3.append(copies.start(sb2.at[at], rb3.at[r - 1], to))
    for copy in g2:
        copy.wait_recv()
    sg2[...] = add_up(sg1[:, x], rg2, X - 1).astype(jnp.bfloat16)
    g3 = []
    for r in rest("z"):
        to, at = place.along("z", r)
        g3.append(copies.start(sg2.at[at], rg3.at[r - 1], to))
    for copy in a2:
        copy.wait_recv()
    sa2[...] = add_up(sa1[yh, :, yl], ra2, Y - 1).astype(jnp.bfloat16)
    a3 = []
    for r in rest("x"):
        to, at = place.along("x", r)
        a3.append(copies.start(sa2.at[at], ra3.at[r - 1], to))

    iswap.wait_recv()
    for b in range(16):
        block = slice(b * 128, (b + 1) * 128)
        mine = pl.ds(pl.multiple_of(b * 256 + core * 128, 128), 128)
        theirs = pl.ds(pl.multiple_of(b * 256 + other * 128, 128), 128)
        ig_ref[:, mine] = igs[here, block]
        ig_ref[:, theirs] = igr[:, block]
    leave = pltpu.make_async_copy(ig_ref, ig_hbm, lsem.at[0])
    leave.start()
    for copy in b3:
        copy.wait_recv()
    wgrad_ref[:, 0:256] = add_up(sb2[z], rb3, Z - 1)
    for copy in g3:
        copy.wait_recv()
    wgrad_ref[:, 256:512] = add_up(sg2[z], rg3, Z - 1)
    for copy in a3:
        copy.wait_recv()
    last = add_up(sa2[x], ra3, X - 1)
    wgrad_ref[:, 512:1024] = jnp.dot(
        last, readout[...], precision=HIGH, preferred_element_type=f32
    )
    for stream in streams:
        stream.close()
    copies.close()
    leave.wait()


def reduce(far, near, w, wb, wg, wa, wd, tb, vfull):
    f32, low = jnp.float32, jnp.bfloat16
    return pl.pallas_call(
        reduce_kernel,
        out_shape=(shape((ROWS, 4096)), shape((16, 1024), f32)),
        in_specs=[ANY] * 9,
        out_specs=(ANY, VMEM),
        scratch_shapes=[
            pltpu.VMEM((ROWS, 4096), low),
            pltpu.VMEM((Z, YH, X, YL, 16, 256), low),
            pltpu.VMEM((Z, YH, X, YL, 16, 256), low),
            pltpu.VMEM((Z, YH, X, YL, 16, 384), low),
            pltpu.VMEM((Z, YH, X, YL, 16, 128), low),
            pltpu.VMEM((2 * ROWS, 2048), low),
            pltpu.VMEM((SP, 8, D), f32),
            pltpu.VMEM((WIN - ROWS, KV * D), low),
            pltpu.VMEM((HEADS, WIN), f32),
            pltpu.VMEM((128, KV * D), f32),
            pltpu.VMEM((2, ROWS, KV * D), low),
            pltpu.VMEM((2, ROWS, KV * D), low),
            pltpu.VMEM((ROWS, KV * D), low),
            pltpu.VMEM((ROWS, KV * D), low),
            pltpu.VMEM((2, HEADS, ROWS), f32),
            pltpu.VMEM((2, HEADS, ROWS), f32),
            pltpu.VMEM((HEADS, ROWS), f32),
            pltpu.VMEM((HEADS, ROWS), f32),
            pltpu.VMEM((ROWS, KV * D), f32),
            pltpu.VMEM((HEADS, ROWS), f32),
            pltpu.VMEM((2 * ROWS, 1152), low),
            pltpu.VMEM((Z, YH, X, YL, 16, 256), low),
            pltpu.VMEM((Z, YH, X, YL, 16, 256), low),
            pltpu.VMEM((Z, YH, X, YL, 16, 128), low),
            pltpu.VMEM((X - 1, Z, YH, YL, 16, 256), low),
            pltpu.VMEM((Y - 1, Z, 16, 256), low),
            pltpu.VMEM((Z - 1, 16, 256), low),
            pltpu.VMEM((Y - 1, Z, X, 16, 256), low),
            pltpu.VMEM((X - 1, Z, 16, 256), low),
            pltpu.VMEM((Z - 1, 16, 256), low),
            pltpu.VMEM((Z - 1, YH, X, YL, 16, 128), low),
            pltpu.VMEM((Y - 1, X, 16, 128), low),
            pltpu.VMEM((X - 1, 16, 128), low),
            pltpu.VMEM((Z, YH, YL, 16, 256), low),
            pltpu.VMEM((Z, 16, 256), low),
            pltpu.VMEM((Z, X, 16, 256), low),
            pltpu.VMEM((Z, 16, 256), low),
            pltpu.VMEM((YH, X, YL, 16, 128), low),
            pltpu.VMEM((X, 16, 128), low),
            pltpu.VMEM((2 * ROWS, 2048), low),
            pltpu.VMEM((ROWS, 2048), low),
            pltpu.SemaphoreType.DMA((64,)),
            pltpu.SemaphoreType.DMA((64,)),
            pltpu.SemaphoreType.DMA((10,)),
        ],
        compiler_params=pltpu.CompilerParams(
            collective_id=1, has_side_effects=True, vmem_limit_bytes=60 * 2**20
        ),
    )(far, near, w, wb, wg, wa, wd, tb, vfull)


def hand_over_kernel(a, b, a_out, b_out, a_here, b_here, come, go):
    moves = [(b, b_here, b_out)]
    for k in range(4):
        rows = slice(k * 32, (k + 1) * 32)
        moves.append((a.at[rows, :], a_here.at[rows, :], a_out.at[rows, :]))
    ins = [pltpu.make_async_copy(src, here, come.at[k]) for k, (src, here, _) in enumerate(moves)]
    outs = [pltpu.make_async_copy(here, dst, go.at[k]) for k, (_, here, dst) in enumerate(moves)]
    for move in ins:
        move.start()
    for first, then in zip(ins, outs):
        first.wait()
        then.start()
    for move in outs:
        move.wait()


def hand_over(a, b):
    return pl.pallas_call(
        hand_over_kernel,
        out_shape=(shape(a.shape, a.dtype), shape(b.shape, b.dtype)),
        in_specs=[ANY, ANY],
        out_specs=(ANY, ANY),
        scratch_shapes=[
            pltpu.VMEM(a.shape, a.dtype),
            pltpu.VMEM(b.shape, b.dtype),
            pltpu.SemaphoreType.DMA((5,)),
            pltpu.SemaphoreType.DMA((5,)),
        ],
        compiler_params=pltpu.CompilerParams(vmem_limit_bytes=60 * 2**20),
    )(a, b)


def on_device(tokens, queries, kv_weight, vhm, lengths, positions, returns):
    vhm = vhm.reshape(HEADS // SP, D)
    kwin, vwin, vfull, wb, wg, wa, wd, tb = gather(tokens, kv_weight, vhm)
    dq, far, near, w = attention(lengths, positions, returns, queries, kwin, vwin, vfull)
    input_grad, weight_grad = reduce(far, near, w, wb, wg, wa, wd, tb, vfull)
    return (dq, *hand_over(input_grad, weight_grad))


def solution(mesh):
    rows = P(("fsdp", "sp"), None)
    slab = P("fsdp", None)
    return jax.shard_map(
        on_device,
        mesh=mesh,
        in_specs=(rows, rows, rows, P("sp"), slab, slab, slab),
        out_specs=(rows, rows, rows),
        check_vma=False,
    )
```
